32 devices in a mesh: grp: 2 (over y), row: 4 (over z), col: 2 (over x), evt: 2 (over core).
Axes of the slice: x: 2, y: 2, z: 4, core: 2. Of those that a mesh axis runs over, the one named last changes fastest.
Arguments:
- sections: float32 [4, 4096], P('evt', ('grp', 'row', 'col')), parts along dimension 1, may hold values from 6.5 to 8.5
- send_list: int32 [8, 2, 4, 64], P(('grp', 'row'), 'col'), parts along dimension 0, may hold values from 0 to 255
- send_count: int32 [8, 2, 4], P(('grp', 'row'), 'col'), parts along dimension 0, may hold values from 32 to 64, as said below
- slot_sender_position: int32 [8, 2, 32], P(('grp', 'row'), 'col'), parts along dimension 0, may hold values from 0 to 255
- block_slot_index: int32 [32, 16], P(('grp', 'row'), 'col'), parts along dimension 0, may hold values from 0 to 31
- hand: float32 [256, 2048], P(('grp', 'row'), 'col'), parts along dimension 0, may hold values from 0.2 to 12
- drain: float32 [256, 2048], P(('grp', 'row'), 'col'), parts along dimension 0, may hold values from 0 to 1.5
- manning: float32 [256, 2048], P(('grp', 'row'), 'col'), parts along dimension 0, may hold values from 0.03 to 0.2
Outputs:
- hand_depth: float32 [4, 256, 2048], P('evt', ('grp', 'row'), 'col'), parts along dimension 1
- final_depth: float32 [4, 256, 2048], P('evt', ('grp', 'row'), 'col'), parts along dimension 1
The draws below stay inside these ranges and needn't reach their ends.
There are 2 independent parts, one for each index of `grp`. The reference program is written for one: setup_inputs(seed, part) draws one part's arguments, and reference() takes and returns one part's arrays. A program takes and returns all parts, laid end to end along the dimension named above; each array names one. Nothing has to cross between parts.
Inputs may be any that keep to these rules, and one draw needn't show every extreme that they name: `send_count`: in every draw some owner's list to some tile row is live in all 64 entries.
All inputs are finite; a program needn't handle non-finite values.
Results may differ from the reference program's by a relative error of at most 0.0002.
Values sent between devices are 32-bit elements; how exact they have to be, the bound alone decides.
A program may use at most 64 MiB of HBM per device.

```python
import math
import jax
import jax.numpy as jnp

CR = 32
CC = 1024
STEPS = 16
SLOT_COUNT = 32
SEND_ENTRIES = 64
CATCH_DEV = 256
BLOCK_ROW_COUNT = 8
BLOCK_COLUMNS = 128
GRID_ROWS = 128
GRID_COLUMNS = 2048
EVENTS = 4
CATCH = 2048
N_ROW = 4
N_COL = 2


def draw_send_count(key, part):
    key_small, key_full, key_spot = jax.random.split(jax.random.fold_in(key, 17), 3)
    total = N_ROW * N_COL * N_ROW
    small_counts = jax.random.randint(key_small, (total,), SEND_ENTRIES // 2, SEND_ENTRIES + 1)
    full_lists = jax.random.randint(key_full, (total,), 0, 2) == 0
    counts = jnp.where(full_lists, SEND_ENTRIES, small_counts)
    spot = jax.random.randint(key_spot, (), 0, total)
    counts = jnp.where(jnp.arange(total, dtype=jnp.int32) == spot, SEND_ENTRIES, counts)
    return counts.reshape(N_ROW, N_COL, N_ROW).astype(jnp.int32)


def draw_hand(key, part):
    key_low, key_high, key_pick = jax.random.split(jax.random.fold_in(key, 29), 3)
    grid_shape = (GRID_ROWS, GRID_COLUMNS)
    draw_one = jax.random.uniform(key_low, grid_shape, jnp.float32)
    draw_two = jax.random.uniform(key_high, grid_shape, jnp.float32)
    draw_three = jax.random.uniform(key_pick, grid_shape, jnp.float32)
    shallow_cells = 0.2 * jnp.exp(jnp.log(5.0) * draw_one)
    steep_cells = jnp.exp(jnp.log(12.0) * draw_two)
    high_share = 0.1
    return jnp.where(draw_three < high_share, steep_cells, shallow_cells).astype(jnp.float32)


def plant(result, own_key, least, top_value):
    dims = result.shape
    spot = [jax.random.randint(jax.random.fold_in(own_key, axis), (), 0, dims[axis]) for axis in range(len(dims))]
    result = result.at[tuple(spot)].set(least)
    longest = dims.index(max(dims))
    spot[longest] = (spot[longest] + 1) % dims[longest]
    return result.at[tuple(spot)].set(top_value)


def levels(key, extent, shards, low, largest):
    def one(dim, shards_of):
        heights = jax.random.uniform(jax.random.fold_in(jax.random.fold_in(key, 6), dim), (shards_of,), jnp.float32, low / len(shards), largest / len(shards))
        return jnp.repeat(jnp.exp(heights), extent[dim] // shards_of).reshape((-1,) + (1,) * (len(extent) - dim - 1))

    level = one(*shards[0])
    for cut in shards[1:]:
        level = level * one(*cut)
    return level


def setup_inputs(seed: int = 0, part: int = 0) -> dict:
    keys = jax.random.split(jax.random.key(seed), 9)
    part_splits = jax.random.split(jax.random.fold_in(keys[8], part), 9)
    sections = jnp.clip(6.5 + 2.0 * jax.random.uniform(part_splits[0], (EVENTS, CATCH), jnp.float32) ** levels(part_splits[0], (EVENTS, CATCH), ((0, 2), (1, 8)), -0.2, 0.2), 6.5, 8.5)
    send_list = plant(jax.random.randint(part_splits[1], (N_ROW, N_COL, N_ROW, SEND_ENTRIES), 0, CATCH_DEV), jax.random.fold_in(part_splits[1], 1), 0, CATCH_DEV - 1).astype(jnp.int32)
    send_count = draw_send_count(jax.random.fold_in(jax.random.fold_in(keys[8], part), 71), part)
    slot_sender_position = plant(jax.random.randint(part_splits[3], (N_ROW, N_COL, SLOT_COUNT), 0, N_ROW * SEND_ENTRIES), jax.random.fold_in(part_splits[3], 1), 0, (N_ROW * SEND_ENTRIES) - 1).astype(jnp.int32)
    block_slot_index = plant(jax.random.randint(part_splits[4], (GRID_ROWS // BLOCK_ROW_COUNT, GRID_COLUMNS // BLOCK_COLUMNS), 0, SLOT_COUNT), jax.random.fold_in(part_splits[4], 1), 0, SLOT_COUNT - 1).astype(jnp.int32)
    hand = draw_hand(jax.random.fold_in(jax.random.fold_in(keys[8], part), 71), part)
    drain = jnp.clip(1.5 * jax.random.uniform(part_splits[6], (GRID_ROWS, GRID_COLUMNS), jnp.float32) ** levels(part_splits[6], (GRID_ROWS, GRID_COLUMNS), ((0, 4), (1, 2)), -0.2, 0.2), 0.0, 1.5)
    manning = jnp.clip(jnp.exp(math.log(0.2) - 1.89712 * jax.random.uniform(part_splits[7], (GRID_ROWS, GRID_COLUMNS), jnp.float32) ** levels(part_splits[7], (GRID_ROWS, GRID_COLUMNS), ((0, 4), (1, 2)), -0.2, 0.2)), 0.03, 0.2)
    return dict(sections=sections, send_list=send_list, send_count=send_count, slot_sender_position=slot_sender_position, block_slot_index=block_slot_index, hand=hand, drain=drain, manning=manning)


GRAVITY = 9.81
TIMESTEP = 0.4
SPACING = 10.0
DEPTH_FLOOR = 0.05
DRY_SECTION = -1000.0


def advance(water_depth, flow_east, flow_south, bed_level, manning):
    surface = water_depth + bed_level
    west_side = surface[:, :, :-1]
    east_side = surface[:, :, 1:]
    face_east = jnp.maximum(west_side, east_side) - jnp.maximum(bed_level[:, :-1], bed_level[:, 1:])
    old_east = flow_east[:, :, :-1]
    rough_east = manning[:, :-1] * manning[:, :-1]
    drag_east = GRAVITY * TIMESTEP * rough_east * jnp.abs(old_east) / jnp.maximum(face_east, DEPTH_FLOOR) ** (7.0 / 3.0)
    new_east = (old_east - GRAVITY * TIMESTEP * face_east * (east_side - west_side) / SPACING) / (1.0 + drag_east)
    north_side = surface[:, :-1, :]
    south_side = surface[:, 1:, :]
    face_south = jnp.maximum(north_side, south_side) - jnp.maximum(bed_level[:-1, :], bed_level[1:, :])
    old_south = flow_south[:, :-1, :]
    rough_south = manning[:-1, :] * manning[:-1, :]
    drag_south = GRAVITY * TIMESTEP * rough_south * jnp.abs(old_south) / jnp.maximum(face_south, DEPTH_FLOOR) ** (7.0 / 3.0)
    new_south = (old_south - GRAVITY * TIMESTEP * face_south * (south_side - north_side) / SPACING) / (1.0 + drag_south)
    change = new_east[:, 1:-1, :-1] - new_east[:, 1:-1, 1:] + new_south[:, :-1, 1:-1] - new_south[:, 1:, 1:-1]
    new_depth = jnp.maximum(water_depth[:, 1:-1, 1:-1] + (TIMESTEP / SPACING) * change, 0.0)
    return new_depth, new_east[:, 1:-1, 1:], new_south[:, 1:, 1:-1]


def reference(sections, send_list, send_count, slot_sender_position, block_slot_index, hand, drain, manning):
    source_row = slot_sender_position // SEND_ENTRIES
    position = slot_sender_position % SEND_ENTRIES
    row_ids = jnp.arange(N_ROW, dtype=jnp.int32)[:, None, None]
    col_ids = jnp.arange(N_COL, dtype=jnp.int32)[None, :, None]
    live_count = send_count[source_row, col_ids, row_ids]
    local_ids = send_list[source_row, col_ids, row_ids, position]
    global_ids = (source_row * N_COL + col_ids) * CATCH_DEV + local_ids
    slot_section = jnp.where((position < live_count)[None], sections[:, global_ids], jnp.float32(DRY_SECTION))
    tile_of_row = jnp.arange(GRID_ROWS // BLOCK_ROW_COUNT, dtype=jnp.int32) // (CR // BLOCK_ROW_COUNT)
    tile_of_col = jnp.arange(GRID_COLUMNS // BLOCK_COLUMNS, dtype=jnp.int32) // (CC // BLOCK_COLUMNS)
    block_section = slot_section[:, tile_of_row[:, None], tile_of_col[None, :], block_slot_index]
    section_cells = jnp.repeat(jnp.repeat(block_section, BLOCK_ROW_COUNT, axis=1), BLOCK_COLUMNS, axis=2)
    hand_depth = jnp.maximum(section_cells - hand[None], 0.0)
    bed_level = jnp.pad(hand + drain, ((1, 1), (1, 1)))
    rough_pad = jnp.pad(manning, ((1, 1), (1, 1)))
    water_depth = hand_depth
    flow_east = jnp.zeros_like(hand_depth)
    flow_south = jnp.zeros_like(hand_depth)
    spacing = ((0, 0), (1, 1), (1, 1))
    for turn in range(STEPS):
        water_depth, flow_east, flow_south = advance(jnp.pad(water_depth, spacing), jnp.pad(flow_east, spacing), jnp.pad(flow_south, spacing), bed_level, rough_pad)
    return hand_depth, water_depth
```

```python
import functools

import jax
import jax.numpy as jnp
from jax import lax
from jax.experimental import pallas as pl
from jax.experimental.pallas import tpu as pltpu
from jax.sharding import PartitionSpec as P

STEPS = 16
GRAVITY = 9.81
TIMESTEP = 0.4
SPACING = 10.0
DEPTH_FLOOR = 0.05
DRY_SECTION = -1000.0

VMEM_BYTES = 24 * 1024 * 1024
LANES = 128
SUBLANES = 8
HALO = STEPS
META_ROWS = 8
SSP_ROW = 3
BSI_ROW = 4
SCALE = GRAVITY * TIMESTEP * TIMESTEP / (SPACING * SPACING)
DRAG_SCALE = (
    GRAVITY * TIMESTEP * SCALE ** (7.0 / 3.0) / (SCALE * TIMESTEP / SPACING)
)
REGIONS = tuple(
    (dr, dc) for dr in (-1, 0, 1) for dc in (-1, 0, 1) if (dr, dc) != (0, 0)
)


def row_spans(dr, tile_rows):
    if dr == -1:
        return pl.ds(tile_rows - HALO, HALO), pl.ds(tile_rows + HALO, HALO)
    if dr == 1:
        return pl.ds(0, HALO), pl.ds(tile_rows, HALO)
    return pl.ds(0, tile_rows), pl.ds(0, tile_rows)


def col_spans(dc, tile_cols):
    if dc == -1:
        return pl.ds(tile_cols - LANES, LANES), pl.ds(tile_cols + LANES, LANES)
    if dc == 1:
        return pl.ds(0, LANES), pl.ds(tile_cols, LANES)
    return pl.ds(0, tile_cols), pl.ds(0, tile_cols)


def flood_kernel(
    row_total, col_total,
    sections_in, send_list_in, send_count_in, slot_position_in, block_slot_in, hand, drain, manning,
    hand_depth, final_depth,
    sections, send_list, send_count, slot_position, block_slot, small_sem,
    ext, meta, meta_levels, landed, landed_levels, table, table_levels,
    depth, east, south, bed, top_east, top_south, drag,
    strip_send, strip_recv, meta_send, meta_recv, own_sem, meta_own_sem, table_sem,
):
    r = lax.axis_index("row")
    k = lax.axis_index("col")
    tile_rows, tile_cols = hand.shape
    events, catch_local = sections.shape
    capacity = send_list.shape[3]
    block_rows, block_cols = block_slot.shape
    width = depth.shape[2]
    tiles = depth.shape[1] // SUBLANES
    halo_tiles = HALO // SUBLANES
    own_tiles = tile_rows // SUBLANES
    halves = catch_local // LANES
    terrain = (hand, drain, manning)

    def col_exists(dc):
        return jnp.logical_and(k + dc >= 0, k + dc < col_total)

    def partner(rr, dc):
        if dc == 0:
            return rr != r
        return col_exists(dc)

    barrier = pltpu.get_barrier_semaphore()
    for rr in range(row_total):
        for dc in (-1, 0, 1):
            @pl.when(partner(rr, dc))
            def _():
                pl.semaphore_signal(
                    barrier, inc=1, device_id={"row": rr, "col": k + dc},
                    device_id_type=pl.DeviceIdType.MESH,
                )

    own_copies = [
        pltpu.make_async_copy(
            terrain[array], ext.at[array, pl.ds(0, tile_rows), pl.ds(0, tile_cols)],
            own_sem.at[array],
        )
        for array in range(3)
    ]
    small_copies = [
        pltpu.make_async_copy(source, target, small_sem.at[at])
        for at, (source, target) in enumerate((
            (sections_in, sections), (send_list_in, send_list), (send_count_in, send_count),
            (slot_position_in, slot_position), (block_slot_in, block_slot),
        ))
    ]
    for copy in small_copies + own_copies:
        copy.start()
    for copy in small_copies:
        copy.wait()

    lane_of = lax.broadcasted_iota(jnp.int32, (1, capacity), 1)
    lists = []
    for rr in range(row_total):
        live = lane_of < jnp.broadcast_to(send_count[0, :, rr : rr + 1], (1, capacity))
        lists.append(jnp.where(live, send_list[0, 0, rr : rr + 1, :], -1))
    slots_held = slot_position[0]
    blocks = block_slot[...]
    for rr in range(row_total):
        meta[rr] = jnp.zeros((META_ROWS, LANES), jnp.int32)
        for j in (-1, 0, 1):
            pick = min(max(rr + j, 0), row_total - 1)
            meta[rr, j + 1 : j + 2, 0:capacity] = lists[pick]
        meta[rr, SSP_ROW : SSP_ROW + 1, 0 : slots_held.shape[1]] = slots_held
        meta[rr, BSI_ROW : BSI_ROW + block_rows, 0:block_cols] = blocks
    for e in range(events):
        for half in range(halves):
            at = e * halves + half
            meta_levels[at : at + 1, :] = sections[e : e + 1, half * LANES : (half + 1) * LANES]

    cols_seen = 1 + (k > 0).astype(jnp.int32) + (k < col_total - 1).astype(jnp.int32)
    pl.semaphore_wait(barrier, row_total * cols_seen - 1)

    def meta_copies(rr, dc, arriving):
        at = (rr, 1 + dc) if arriving else (r, 1 - dc)
        return [
            pltpu.make_async_remote_copy(
                src_ref=source,
                dst_ref=target.at[at],
                send_sem=meta_send.at[which, rr, dc + 1],
                recv_sem=meta_recv.at[(which,) + at],
                device_id={"row": rr, "col": k + dc},
                device_id_type=pl.DeviceIdType.MESH,
            )
            for which, (source, target) in enumerate(
                ((meta.at[rr], landed), (meta_levels, landed_levels))
            )
        ]

    def strip_copy(index, array, dr, dc):
        src_rows, dst_rows = row_spans(dr, tile_rows)
        src_cols, dst_cols = col_spans(dc, tile_cols)
        source = terrain[array]
        return pltpu.make_async_remote_copy(
            src_ref=source.at[src_rows, src_cols],
            dst_ref=ext.at[array, dst_rows, dst_cols],
            send_sem=strip_send.at[index, array],
            recv_sem=strip_recv.at[index, array],
            device_id={"row": r - dr, "col": k - dc},
            device_id_type=pl.DeviceIdType.MESH,
        )

    def tile_exists(dr, dc):
        there = jnp.logical_and(r + dr >= 0, r + dr < row_total)
        return jnp.logical_and(there, col_exists(dc))

    for rr in range(row_total):
        for dc in (-1, 0, 1):
            @pl.when(partner(rr, dc))
            def _():
                for copy in meta_copies(rr, dc, False):
                    copy.start()
    for index, (dr, dc) in enumerate(REGIONS):
        @pl.when(tile_exists(-dr, -dc))
        def _():
            for array in range(3):
                strip_copy(index, array, dr, dc).start()
    meta_own = [
        pltpu.make_async_copy(meta.at[r], landed.at[r, 1], meta_own_sem.at[0]),
        pltpu.make_async_copy(meta_levels, landed_levels.at[r, 1], meta_own_sem.at[1]),
    ]
    for copy in meta_own:
        copy.start()

    lane = lax.broadcasted_iota(jnp.int32, (SUBLANES, LANES), 1)
    near = lane < LANES // 2
    has_east = k < col_total - 1
    has_west = k > 0
    has_north = r > 0
    has_south = r < row_total - 1

    def section(dr, kc, row, col):
        rr = jnp.clip(r + dr, 0, row_total - 1)
        slot = table[rr, kc, BSI_ROW + row, col]
        place = table[rr, kc, SSP_ROW, slot]
        src = place // capacity
        local = table[src, kc, dr + 1, place % capacity]
        pick = jnp.maximum(local, 0)
        return [
            jnp.where(
                local >= 0,
                table_levels[src, kc, e * halves + pick // LANES, pick % LANES],
                jnp.float32(DRY_SECTION),
            )
            for e in range(events)
        ]

    lane_ok = jnp.where(near, has_east.astype(jnp.int32), has_west.astype(jnp.int32)) > 0

    row_id = lax.broadcasted_iota(jnp.int32, (SUBLANES, LANES), 0)
    upper = row_id < SUBLANES // 2

    south_near = own_tiles

    def tile_place(t):
        if t < own_tiles:
            return 0, t
        if t < own_tiles + halo_tiles:
            return 1, t - own_tiles
        return -1, t - halo_tiles - halo_tiles

    def inside(flag):
        return jnp.broadcast_to(flag.astype(jnp.int32), (SUBLANES, LANES))

    def keep_of(t, seam=False):
        dr = tile_place(t)[0]
        if seam:
            full = jnp.where(upper, inside(has_south), inside(has_north)) > 0
        elif dr == 0:
            return None, lane_ok
        else:
            full = inside(has_south if dr == 1 else has_north) > 0
        return full, jnp.logical_and(full, lane_ok)

    def masked(x, t, seam=False):
        full, side = keep_of(t, seam)
        body = x[:, :tile_cols]
        tail = jnp.where(side, x[:, tile_cols:], 0.0)
        if full is not None:
            body = jnp.where(jnp.concatenate([full] * (tile_cols // LANES), 1), body, 0.0)
        return jnp.concatenate([body, tail], 1)

    def span(t):
        return pl.ds(t * SUBLANES, SUBLANES)

    def beside(array, t):
        return jnp.where(
            near,
            ext[array, span(t), tile_cols : tile_cols + LANES],
            ext[array, span(t), tile_cols + LANES : tile_cols + 2 * LANES],
        )

    def keep(mask, x):
        return x if mask is None else jnp.where(mask, x, 0.0)

    def repeated(mask):
        return None if mask is None else jnp.concatenate([mask] * (tile_cols // LANES), 1)

    def set_terrain(t, mask, values, lanes):
        height, low, rough = values
        bed[span(t), lanes] = keep(mask, SCALE * (height + low))
        drag[span(t), lanes] = keep(mask, DRAG_SCALE * (rough * rough))

    main = slice(0, tile_cols)
    side = slice(tile_cols, width)

    def set_main(t):
        mask = repeated(keep_of(t)[0])
        set_terrain(t, mask, [ext[array, span(t), main] for array in range(3)], main)

    def set_depth(t):
        dr, row = tile_place(t)
        mask = keep_of(t)[0]
        for col in range(block_cols):
            lanes = slice(col * LANES, (col + 1) * LANES)
            height = ext[0, span(t), lanes]
            for e, level in enumerate(section(dr, 1, row, col)):
                value = SCALE * jnp.maximum(level - height, 0.0)
                if dr == 0:
                    hand_depth[e, span(t), lanes] = value
                depth[e, span(t), lanes] = keep(mask, value)

    for t in range(tiles):
        for e in range(events):
            east[e, span(t), :] = jnp.zeros((SUBLANES, width), jnp.float32)
            south[e, span(t), :] = jnp.zeros((SUBLANES, width), jnp.float32)
    for copy in own_copies:
        copy.wait()
    for t in range(own_tiles):
        set_main(t)

    for copy in meta_own:
        copy.wait()
    for rr in range(row_total):
        for dc in (-1, 0, 1):
            @pl.when(partner(rr, dc))
            def _():
                for copy in meta_copies(rr, dc, True):
                    copy.wait_recv()
    tables = []
    for kc in range(3):
        held = 1 if kc == 1 else jnp.where(col_exists(kc - 1), kc, 1)
        for which, (source, target) in enumerate(
            ((landed, table), (landed_levels, table_levels))
        ):
            tables.append(
                pltpu.make_async_copy(
                    source.at[:, held], target.at[:, kc], table_sem.at[which, kc]
                )
            )
    for copy in tables:
        copy.start()
    for copy in tables:
        copy.wait()
    for t in range(own_tiles):
        set_depth(t)

    side_levels = []
    for t in range(tiles):
        dr, row = tile_place(t)
        side_levels.append((section(dr, 2, row, 0), section(dr, 0, row, block_cols - 1)))

    for index, (dr, dc) in enumerate(REGIONS):
        @pl.when(tile_exists(dr, dc))
        def _():
            for array in range(3):
                strip_copy(index, array, dr, dc).wait_recv()
    for t in range(own_tiles, tiles):
        set_main(t)
        set_depth(t)
    for t in range(tiles):
        mask = keep_of(t)[1]
        values = [beside(array, t) for array in range(3)]
        set_terrain(t, mask, values, side)
        for e in range(events):
            level = jnp.where(near, side_levels[t][0][e], side_levels[t][1][e])
            depth[e, span(t), side] = keep(
                mask, SCALE * jnp.maximum(level - values[0], 0.0)
            )

    wide_row = lax.broadcasted_iota(jnp.int32, (SUBLANES, width), 0)
    last_row = wide_row == SUBLANES - 1
    first_row = wide_row == 0

    def up(x):
        return pltpu.roll(x, SUBLANES - 1, 0)

    def down(x):
        return pltpu.roll(x, 1, 0)

    def left(x):
        return pltpu.roll(x, width - 1, 1)

    def right(x):
        return pltpu.roll(x, 1, 1)

    for t in range(tiles):
        here = bed[span(t), :]
        after = bed[span((t + 1) % tiles), :]
        top_east[span(t), :] = jnp.maximum(here, left(here))
        top_south[span(t), :] = jnp.maximum(here, jnp.where(last_row, up(after), up(here)))

    def face(flow, here, beyond, top, rough):
        thick = jnp.maximum(here, beyond) - top
        power = jnp.exp2((-7.0 / 3.0) * jnp.log2(jnp.maximum(thick, SCALE * DEPTH_FLOOR)))
        pushed = flow - thick * (beyond - here)
        return pushed * pl.reciprocal(1.0 + rough * jnp.abs(flow) * power, approx=True)

    def step_ring(ring, seam):
        last = ring[-1]
        for e in range(events):
            def level(t):
                water = depth[e, span(t), :]
                here = water + bed[span(t), :]
                return water, here, up(here)

            def go_south(t, here, here_up, next_up):
                return face(
                    south[e, span(t), :], here, jnp.where(last_row, next_up, here_up),
                    top_south[span(t), :], drag[span(t), :],
                )

            final = level(last)
            now = level(ring[0])
            final_south = go_south(last, final[1], final[2], now[2])
            south_above = down(final_south)
            for place, t in enumerate(ring):
                water, here, here_up = now
                if t == last:
                    new_south = final_south
                else:
                    after = ring[place + 1]
                    now = final if after == last else level(after)
                    new_south = go_south(t, here, here_up, now[2])
                new_east = face(
                    east[e, span(t), :], here, left(here), top_east[span(t), :], drag[span(t), :]
                )
                south_down = down(new_south)
                change = (right(new_east) - new_east) + (
                    jnp.where(first_row, south_above, south_down) - new_south
                )
                depth[e, span(t), :] = masked(jnp.maximum(water + change, 0.0), t, t == seam)
                east[e, span(t), :] = masked(new_east, t, t == seam)
                south[e, span(t), :] = masked(new_south, t, t == seam)
                south_above = south_down

    def merge(near_tile, far_tile):
        half = wide_row < SUBLANES // 2
        for ref in (bed, top_east, top_south, drag):
            ref[span(near_tile), :] = jnp.where(half, ref[span(near_tile), :], ref[span(far_tile), :])
        for ref in (depth, east, south):
            for e in range(events):
                ref[e, span(near_tile), :] = jnp.where(
                    half, ref[e, span(near_tile), :], ref[e, span(far_tile), :]
                )

    def run(ring, seam):
        def one(turn, carry):
            step_ring(ring, seam)
            return carry

        lax.fori_loop(0, SUBLANES // 2, one, 0)

    slots = list(range(tiles))
    for depth_tiles in range(halo_tiles, 0, -1):
        souths = slots[south_near : south_near + depth_tiles]
        norths = slots[tiles - depth_tiles :]
        own = slots[:own_tiles]
        run(own + souths + norths, None)
        merge(souths[-1], norths[0])
        run(own + souths + norths[1:], souths[-1])

    for e in range(events):
        final_depth[e] = depth[e, 0:tile_rows, 0:tile_cols]

    for index, (dr, dc) in enumerate(REGIONS):
        @pl.when(tile_exists(-dr, -dc))
        def _():
            for array in range(3):
                strip_copy(index, array, dr, dc).wait_send()
    for rr in range(row_total):
        for dc in (-1, 0, 1):
            @pl.when(partner(rr, dc))
            def _():
                for copy in meta_copies(rr, dc, False):
                    copy.wait_send()


def body(
    row_total, col_total,
    sections, send_list, send_count, slot_sender_position, block_slot_index, hand, drain, manning,
):
    events, catch_local = sections.shape
    tile_rows, tile_cols = hand.shape
    vmem = pl.BlockSpec(memory_space=pltpu.VMEM)
    hbm = pl.BlockSpec(memory_space=pltpu.HBM)
    padded_rows = tile_rows + 2 * HALO
    width = tile_cols + LANES
    level_rows = events * (catch_local // LANES)
    state = pltpu.VMEM((events, padded_rows, width), jnp.float32)
    fixed = pltpu.VMEM((padded_rows, width), jnp.float32)
    out = jax.ShapeDtypeStruct((events, tile_rows, tile_cols), jnp.float32)
    landing = (row_total, 3, META_ROWS, LANES)
    landing_levels = (row_total, 3, level_rows, LANES)
    start, end = pl.pallas_call(
        functools.partial(flood_kernel, row_total, col_total),
        out_shape=(out, out),
        in_specs=[hbm] * 8,
        out_specs=(vmem, vmem),
        scratch_shapes=[
            pltpu.VMEM(x.shape, x.dtype)
            for x in (sections, send_list, send_count, slot_sender_position, block_slot_index)
        ]
        + [pltpu.SemaphoreType.DMA((5,))]
        + [
            pltpu.VMEM((3, padded_rows, tile_cols + 2 * LANES), jnp.float32),
            pltpu.VMEM((row_total, META_ROWS, LANES), jnp.int32),
            pltpu.VMEM((level_rows, LANES), jnp.float32),
            pltpu.VMEM(landing, jnp.int32),
            pltpu.VMEM(landing_levels, jnp.float32),
            pltpu.SMEM(landing, jnp.int32),
            pltpu.SMEM(landing_levels, jnp.float32),
        ]
        + [state] * 3
        + [fixed] * 4
        + [
            pltpu.SemaphoreType.DMA((len(REGIONS), 3)),
            pltpu.SemaphoreType.DMA((len(REGIONS), 3)),
            pltpu.SemaphoreType.DMA((2, row_total, 3)),
            pltpu.SemaphoreType.DMA((2, row_total, 3)),
            pltpu.SemaphoreType.DMA((3,)),
            pltpu.SemaphoreType.DMA((2,)),
            pltpu.SemaphoreType.DMA((2, 3)),
        ],
        compiler_params=pltpu.CompilerParams(
            collective_id=0, has_side_effects=True, vmem_limit_bytes=VMEM_BYTES
        ),
        name="flood",
    )(*[
        pltpu.with_memory_space_constraint(x, pltpu.HBM)
        for x in (
            sections, send_list, send_count, slot_sender_position, block_slot_index, hand, drain, manning,
        )
    ])
    return start * (1.0 / SCALE), end * (1.0 / SCALE)


def solution(mesh):
    return jax.shard_map(
        functools.partial(body, mesh.shape["row"], mesh.shape["col"]),
        mesh=mesh,
        in_specs=(
            P("evt", ("grp", "row", "col")),
            P(("grp", "row"), "col", None, None),
            P(("grp", "row"), "col", None),
            P(("grp", "row"), "col", None),
            P(("grp", "row"), "col"),
            P(("grp", "row"), "col"),
            P(("grp", "row"), "col"),
            P(("grp", "row"), "col"),
        ),
        out_specs=(P("evt", ("grp", "row"), "col"), P("evt", ("grp", "row"), "col")),
        check_vma=False,
    )
```

```python
import functools

import jax
import jax.numpy as jnp
from jax import lax
from jax.experimental import pallas as pl
from jax.experimental.pallas import tpu as pltpu
from jax.sharding import PartitionSpec as P

STEPS = 16
GRAVITY = 9.81
TIMESTEP = 0.4
SPACING = 10.0
DEPTH_FLOOR = 0.05
DRY_SECTION = -1000.0

VMEM_BYTES = 24 * 1024 * 1024
LANES = 128
SUBLANES = 8
HALO = STEPS
SCALE = GRAVITY * TIMESTEP * TIMESTEP / (SPACING * SPACING)
DRAG_SCALE = (
    GRAVITY * TIMESTEP * SCALE ** (7.0 / 3.0) / (SCALE * TIMESTEP / SPACING)
)
REGIONS = tuple(
    (dr, dc) for dr in (-1, 0, 1) for dc in (-1, 0, 1) if (dr, dc) != (0, 0)
)
EDGE_STEPS = ((6, 7), (5, 9))
INNER_STEPS = ((8, 3), (7, 4), (6, 4), (5, 5))


def phases(has_north, has_south, own_tiles):
    if has_north and has_south:
        return [
            (-(tiles - own_tiles) * SUBLANES // 2, tiles, steps) for tiles, steps in INNER_STEPS
        ]
    return [
        (-(tiles - own_tiles) * SUBLANES if has_north else 0, tiles, steps)
        for tiles, steps in EDGE_STEPS
    ]


def row_spans(dr, tile_rows):
    if dr == -1:
        return pl.ds(tile_rows - HALO, HALO), pl.ds(0, HALO)
    if dr == 1:
        return pl.ds(0, HALO), pl.ds(HALO + tile_rows, HALO)
    return pl.ds(0, tile_rows), pl.ds(HALO, tile_rows)


def col_spans(dc, tile_cols):
    if dc == -1:
        return pl.ds(tile_cols - LANES, LANES), pl.ds(tile_cols + LANES, LANES)
    if dc == 1:
        return pl.ds(0, LANES), pl.ds(tile_cols, LANES)
    return pl.ds(0, tile_cols), pl.ds(0, tile_cols)


def pick_lanes(x, index):
    return jnp.take_along_axis(x, index, axis=1, mode="promise_in_bounds")


def flood_kernel(
    row_total, col_total,
    sections_in, send_list_in, send_count_in, slot_position_in, block_slot_in, hand, drain, manning,
    hand_depth, final_depth,
    sections, send_list, send_count, slot_position, block_slot,
    ext, lists, flat, slots, message, landed, place, where_held,
    bed_rows, drag_rows, rows, surface, east, south, fixed,
    small_sem, own_sem, strip_send, strip_recv, level_send, level_recv, place_send, place_recv, later_sem,
):
    r = lax.axis_index("row")
    k = lax.axis_index("col")
    tile_rows, tile_cols = hand.shape
    events, catch_local = sections.shape
    capacity = send_list.shape[3]
    block_rows, block_cols = block_slot.shape
    blocks = block_rows * block_cols
    cols = tile_cols // LANES
    width = tile_cols + LANES
    own_tiles = tile_rows // SUBLANES
    halo_tiles = HALO // SUBLANES
    terrain = (hand, drain, manning)

    def row_exists(dr):
        return jnp.logical_and(r + dr >= 0, r + dr < row_total)

    def col_exists(dc):
        return jnp.logical_and(k + dc >= 0, k + dc < col_total)

    def tile_exists(dr, dc):
        if dr == 0:
            return col_exists(dc)
        if dc == 0:
            return row_exists(dr)
        return jnp.logical_and(row_exists(dr), col_exists(dc))

    def as_int(flag):
        return flag.astype(jnp.int32)

    earlier = ((-1, -1), (-1, 0), (-1, 1), (0, -1))
    later = ((1, -1), (1, 0), (1, 1), (0, 1))
    barrier = pltpu.get_barrier_semaphore()

    def tell(semaphore, dr, dc):
        pl.semaphore_signal(
            semaphore, inc=1, device_id={"row": r + dr, "col": k + dc},
            device_id_type=pl.DeviceIdType.MESH,
        )

    for dr, dc in later:
        @pl.when(tile_exists(dr, dc))
        def _():
            tell(barrier, dr, dc)

    small_copies = [
        pltpu.make_async_copy(source, target, small_sem.at[at])
        for at, (source, target) in enumerate((
            (sections_in, sections), (send_list_in, send_list), (send_count_in, send_count),
            (slot_position_in, slot_position), (block_slot_in, block_slot),
        ))
    ]
    own_copies = [
        pltpu.make_async_copy(
            terrain[array], ext.at[array, pl.ds(HALO, tile_rows), pl.ds(0, tile_cols)],
            own_sem.at[array],
        )
        for array in range(3)
    ]
    for copy in small_copies + own_copies:
        copy.start()

    lane = lax.broadcasted_iota(jnp.int32, (SUBLANES, LANES), 1)
    row_id = lax.broadcasted_iota(jnp.int32, (SUBLANES, LANES), 0)
    near = lane < LANES // 2
    lists[...] = jnp.zeros(lists.shape, jnp.int32)
    flat[...] = jnp.zeros(flat.shape, jnp.int32)
    slots[...] = jnp.zeros(slots.shape, jnp.int32)
    for copy in small_copies:
        copy.wait()

    lane_of = lax.broadcasted_iota(jnp.int32, (1, capacity), 1)
    for rr in range(row_total):
        live = lane_of < jnp.broadcast_to(send_count[0, :, rr : rr + 1], (1, capacity))
        held = jnp.where(live, send_list[0, 0, rr : rr + 1, :], -1)
        for e in range(events):
            lists[rr : rr + 1, e * capacity : (e + 1) * capacity] = held
    list_rows = lists.shape[0]
    lane_tall = lax.broadcasted_iota(jnp.int32, (list_rows, LANES), 1)
    wanted = lists[...]
    local = jnp.maximum(wanted, 0)
    values = jnp.full((list_rows, LANES), DRY_SECTION, jnp.float32)
    for half in range(catch_local // LANES):
        mine = jnp.logical_and(wanted >= half * LANES, wanted < (half + 1) * LANES)
        for e in range(events):
            source = jnp.broadcast_to(
                sections[e : e + 1, half * LANES : (half + 1) * LANES], (list_rows, LANES)
            )
            found = pick_lanes(source, jnp.bitwise_and(local, LANES - 1))
            of_event = jnp.logical_and(lane_tall >= e * capacity, lane_tall < (e + 1) * capacity)
            values = jnp.where(jnp.logical_and(mine, of_event), found, values)
    for rr in range(row_total):
        message[rr] = jnp.full((SUBLANES, LANES), DRY_SECTION, jnp.float32)
        for j in (-1, 0, 1):
            pick = min(max(rr + j, 0), row_total - 1)
            message[rr, j + 1 : j + 2, :] = values[pick : pick + 1, :]

    ahead = sum(as_int(tile_exists(dr, dc)) for dr, dc in earlier) + as_int(r >= 2)

    @pl.when(ahead > 0)
    def _():
        pl.semaphore_wait(barrier, ahead)

    @pl.when(jnp.logical_and(r >= 1, r + 1 < row_total))
    def _():
        tell(barrier, 1, 0)

    for dr, dc in earlier:
        @pl.when(tile_exists(dr, dc))
        def _():
            tell(later_sem, dr, dc)

    def level_copy(rr, dc, arriving):
        at = (rr, 1 + dc) if arriving else (r, 1 - dc)
        return pltpu.make_async_remote_copy(
            src_ref=message.at[rr],
            dst_ref=landed.at[at],
            send_sem=level_send.at[rr, dc + 1],
            recv_sem=level_recv.at[at],
            device_id={"row": rr, "col": k + dc},
            device_id_type=pl.DeviceIdType.MESH,
        )

    def place_copy(index, dr, dc):
        return pltpu.make_async_remote_copy(
            src_ref=place,
            dst_ref=where_held.at[1 + dr, 1 + dc],
            send_sem=place_send.at[index],
            recv_sem=place_recv.at[index],
            device_id={"row": r - dr, "col": k - dc},
            device_id_type=pl.DeviceIdType.MESH,
        )

    def strip_copy(index, array, dr, dc):
        src_rows, dst_rows = row_spans(dr, tile_rows)
        src_cols, dst_cols = col_spans(dc, tile_cols)
        return pltpu.make_async_remote_copy(
            src_ref=terrain[array].at[src_rows, src_cols],
            dst_ref=ext.at[array, dst_rows, dst_cols],
            send_sem=strip_send.at[index, array],
            recv_sem=strip_recv.at[index, array],
            device_id={"row": r - dr, "col": k - dc},
            device_id_type=pl.DeviceIdType.MESH,
        )

    def send_levels(to_earlier):
        for rr in range(row_total):
            for dc in (-1, 0, 1):
                if to_earlier:
                    there = (rr <= r) if dc == -1 else (rr < r)
                else:
                    there = (rr >= r) if dc == 1 else (rr > r)
                if dc != 0:
                    there = jnp.logical_and(there, col_exists(dc))

                @pl.when(there)
                def _():
                    level_copy(rr, dc, False).start()

    def send_near(targets):
        for index, (dr, dc) in enumerate(REGIONS):
            if (-dr, -dc) in targets:
                @pl.when(tile_exists(-dr, -dc))
                def _():
                    place_copy(index, dr, dc).start()
                    for array in range(3):
                        strip_copy(index, array, dr, dc).start()

    send_levels(True)

    slots[0:1, 0 : slot_position.shape[2]] = slot_position[0]
    for e in range(events):
        for row in range(block_rows):
            at = e * blocks + row * block_cols
            flat[0:1, at : at + block_cols] = block_slot[row : row + 1, :]
    tile_shape = (SUBLANES, LANES)
    own_place = pick_lanes(
        jnp.broadcast_to(slots[0:1, :], tile_shape), jnp.broadcast_to(flat[0:1, :], tile_shape)
    )
    place[...] = own_place
    where_held[1, 1] = own_place

    send_near(earlier)
    behind = sum(as_int(tile_exists(dr, dc)) for dr, dc in later) + as_int(r + 2 < row_total)

    @pl.when(behind > 0)
    def _():
        pl.semaphore_wait(later_sem, behind)

    @pl.when(jnp.logical_and(r >= 1, r + 1 < row_total))
    def _():
        tell(later_sem, -1, 0)

    send_levels(False)
    send_near(later)
    landed[r, 1] = message[r]

    lane_ok = jnp.where(near, as_int(col_exists(1)), as_int(col_exists(-1))) > 0
    wide_row = lax.broadcasted_iota(jnp.int32, (SUBLANES, width), 0)
    last_row = wide_row == SUBLANES - 1
    first_row = wide_row == 0

    def span(t):
        return pl.ds(t * SUBLANES, SUBLANES)

    def piece(j):
        return slice(j * LANES, (j + 1) * LANES)

    def up(x):
        return pltpu.roll(x, SUBLANES - 1, 0)

    def down(x):
        return pltpu.roll(x, 1, 0)

    def left(x):
        return pltpu.roll(x, width - 1, 1)

    def right(x):
        return pltpu.roll(x, 1, 1)

    def guard(x):
        return jnp.concatenate(
            [x[:, :tile_cols], jnp.where(lane_ok, x[:, tile_cols:], 0.0)], 1
        )

    def beside(array, t):
        return jnp.where(
            near,
            ext[array, span(t), tile_cols : tile_cols + LANES],
            ext[array, span(t), tile_cols + LANES : tile_cols + 2 * LANES],
        )

    def set_terrain(t, side):
        if side:
            height, low, rough = [beside(array, t) for array in range(3)]
            bed_rows[cols, span(t), :] = jnp.where(lane_ok, SCALE * (height + low), 0.0)
            drag_rows[cols, span(t), :] = jnp.where(lane_ok, DRAG_SCALE * (rough * rough), 0.0)
            return
        for j in range(cols):
            height, low, rough = [ext[array, span(t), piece(j)] for array in range(3)]
            bed_rows[j, span(t), :] = SCALE * (height + low)
            drag_rows[j, span(t), :] = DRAG_SCALE * (rough * rough)

    def spread(ref, first, tiles, t):
        return jnp.concatenate(
            [ref[j, pl.ds(first + t, SUBLANES, stride=tiles), :] for j in range(cols + 1)], 1
        )

    def gather_back(ref, first, tiles, t, x):
        for j in range(cols + 1):
            ref[j, pl.ds(first + t, SUBLANES, stride=tiles), :] = x[:, piece(j)]

    def level_of(held, dr, lane_at):
        return jnp.broadcast_to(held[dr + 1 : dr + 2, lane_at : lane_at + 1], tile_shape)

    def face(flow, here, beyond, top, rough):
        thick = jnp.maximum(here, beyond) - top
        power = jnp.exp2((-7.0 / 3.0) * jnp.log2(jnp.maximum(thick, SCALE * DEPTH_FLOOR)))
        pushed = flow - thick * (beyond - here)
        return pushed * pl.reciprocal(1.0 + rough * jnp.abs(flow) * power, approx=True)

    def flood(has_north, has_south):
        plan = [(first + HALO, tiles, steps) for first, tiles, steps in phases(has_north, has_south, own_tiles)]
        row_tiles = range(
            0 if has_north else halo_tiles,
            halo_tiles + own_tiles + (halo_tiles if has_south else 0),
        )

        def below(bottom, x):
            x = up(x)
            return x if has_south else jnp.where(last_row, 0.0, x)

        for t in range(halo_tiles, halo_tiles + own_tiles):
            set_terrain(t, False)
        for index, (dr, dc) in enumerate(REGIONS):
            if (dr == -1 and not has_north) or (dr == 1 and not has_south):
                continue

            @pl.when(col_exists(dc))
            def _():
                for array in range(3):
                    strip_copy(index, array, dr, dc).wait_recv()
        for t in row_tiles:
            if t < halo_tiles or t >= halo_tiles + own_tiles:
                set_terrain(t, False)
            set_terrain(t, True)

        base = 0
        for first, tiles, _ in plan:
            start = spread(bed_rows, first, tiles, 0)
            here = start
            for t in range(tiles):
                after = below(True, start) if t == tiles - 1 else spread(bed_rows, first, tiles, t + 1)
                fixed[base + t, 0] = here
                fixed[base + t, 1] = jnp.maximum(here, left(here))
                fixed[base + t, 2] = jnp.maximum(here, after)
                fixed[base + t, 3] = spread(drag_rows, first, tiles, t)
                here = after
            base += tiles
        for t in range(plan[0][1]):
            for e in range(events):
                east[e, t] = jnp.zeros((SUBLANES, width), jnp.float32)
                south[e, t] = jnp.zeros((SUBLANES, width), jnp.float32)

        for index, (dr, dc) in enumerate(REGIONS):
            if (dr == -1 and not has_north) or (dr == 1 and not has_south):
                continue

            @pl.when(col_exists(dc))
            def _():
                place_copy(index, dr, dc).wait_recv()
        for rr in range(row_total):
            for dc in (-1, 0, 1):
                there = (rr != r) if dc == 0 else col_exists(dc)

                @pl.when(there)
                def _():
                    level_copy(rr, dc, True).wait_recv()

        event_shift = jnp.where(lane >= blocks, capacity, 0)
        levels = []
        for kc in range(3):
            placed = jnp.where(
                row_id == 0, where_held[0, kc], jnp.where(row_id == 1, where_held[1, kc], where_held[2, kc])
            )
            source = lax.shift_right_logical(placed, capacity.bit_length() - 1)
            at = jnp.bitwise_and(placed, capacity - 1) + event_shift
            level = jnp.full(tile_shape, DRY_SECTION, jnp.float32)
            for rr in range(row_total):
                level = jnp.where(source == rr, pick_lanes(landed[rr, kc], at), level)
            levels.append(level)

        for t in row_tiles:
            dr, row = 0, t - halo_tiles
            if t < halo_tiles:
                dr, row = -1, block_rows - halo_tiles + t
            elif row >= own_tiles:
                dr, row = 1, row - own_tiles
            side_height = beside(0, t)
            for e in range(events):
                at = e * blocks + row * block_cols
                for j in range(cols):
                    value = SCALE * jnp.maximum(
                        level_of(levels[1], dr, at + j) - ext[0, span(t), piece(j)], 0.0
                    )
                    if dr == 0:
                        hand_depth[e, span(row), piece(j)] = value
                    rows[0, e, j, span(t), :] = value + bed_rows[j, span(t), :]
                level = jnp.where(
                    near, level_of(levels[2], dr, at), level_of(levels[0], dr, at + block_cols - 1)
                )
                value = SCALE * jnp.maximum(level - side_height, 0.0) + bed_rows[cols, span(t), :]
                rows[0, e, cols, span(t), :] = jnp.where(lane_ok, value, 0.0)

        def one_step(base, tiles):
            end = tiles - 1
            for e in range(events):
                def go_south(t, here, beyond):
                    return face(south[e, t], here, beyond, fixed[base + t, 2], fixed[base + t, 3])

                start = surface[e, 0]
                final_south = go_south(end, surface[e, end], below(True, start))
                above = down(final_south)
                if not has_north:
                    above = jnp.where(first_row, (fixed[base, 0] - start) * start, above)
                here = start
                for t in range(tiles):
                    if t == end:
                        new_south = final_south
                        after = None
                    else:
                        after = surface[e, t + 1]
                        new_south = go_south(t, here, after)
                    new_east = face(
                        east[e, t], here, left(here), fixed[base + t, 1], fixed[base + t, 3]
                    )
                    change = (right(new_east) - new_east) + (above - new_south)
                    surface[e, t] = guard(jnp.maximum(here + change, fixed[base + t, 0]))
                    east[e, t] = guard(new_east)
                    south[e, t] = new_south
                    above = new_south
                    here = after

        base = 0
        for number, (first, tiles, steps) in enumerate(plan):
            if number > 0:
                old_first, old_tiles, _ = plan[number - 1]
                for e in range(events):
                    for which, ref in enumerate((surface, east, south)):
                        for t in range(old_tiles):
                            gather_back(rows.at[which, e], old_first, old_tiles, t, ref[e, t])
            for e in range(events):
                for which, ref in enumerate((surface, east, south)):
                    if number > 0 or which == 0:
                        for t in range(tiles):
                            ref[e, t] = spread(rows.at[which, e], first, tiles, t)

            def one(turn, carry, base=base, tiles=tiles):
                one_step(base, tiles)
                return carry

            lax.fori_loop(0, steps, one, 0)
            base += tiles
        first, tiles, _ = plan[-1]
        for e in range(events):
            for t in range(tiles):
                gather_back(rows.at[0, e], first, tiles, t, surface[e, t])
            for t in range(own_tiles):
                for j in range(cols):
                    at = span(halo_tiles + t)
                    final_depth[e, span(t), piece(j)] = rows[0, e, j, at, :] - bed_rows[j, at, :]

    for copy in own_copies:
        copy.wait()

    @pl.when(r == 0)
    def _():
        flood(False, True)

    @pl.when(jnp.logical_and(r > 0, r < row_total - 1))
    def _():
        flood(True, True)

    @pl.when(r == row_total - 1)
    def _():
        flood(True, False)

    for index, (dr, dc) in enumerate(REGIONS):
        @pl.when(tile_exists(-dr, -dc))
        def _():
            place_copy(index, dr, dc).wait_send()
            for array in range(3):
                strip_copy(index, array, dr, dc).wait_send()
    for rr in range(row_total):
        for dc in (-1, 0, 1):
            there = (rr != r) if dc == 0 else col_exists(dc)

            @pl.when(there)
            def _():
                level_copy(rr, dc, False).wait_send()


def body(
    row_total, col_total,
    sections, send_list, send_count, slot_sender_position, block_slot_index, hand, drain, manning,
):
    events = sections.shape[0]
    tile_rows, tile_cols = hand.shape
    vmem = pl.BlockSpec(memory_space=pltpu.VMEM)
    hbm = pl.BlockSpec(memory_space=pltpu.HBM)
    padded_rows = tile_rows + 2 * HALO
    padded_tiles = padded_rows // SUBLANES
    width = tile_cols + LANES
    pieces = width // LANES
    small = (sections, send_list, send_count, slot_sender_position, block_slot_index)
    list_rows = -(-row_total // SUBLANES) * SUBLANES
    fixed_tiles = max(
        sum(tiles for tiles, _ in EDGE_STEPS), sum(tiles for tiles, _ in INNER_STEPS)
    )
    by_rows = pltpu.VMEM((pieces, padded_rows, LANES), jnp.float32)
    state = pltpu.VMEM((events, padded_tiles, SUBLANES, width), jnp.float32)
    out = jax.ShapeDtypeStruct((events, tile_rows, tile_cols), jnp.float32)
    start, end = pl.pallas_call(
        functools.partial(flood_kernel, row_total, col_total),
        out_shape=(out, out),
        in_specs=[hbm] * 8,
        out_specs=(vmem, vmem),
        scratch_shapes=[pltpu.VMEM(x.shape, x.dtype) for x in small]
        + [
            pltpu.VMEM((3, padded_rows, tile_cols + 2 * LANES), jnp.float32),
            pltpu.VMEM((list_rows, LANES), jnp.int32),
            pltpu.VMEM((SUBLANES, LANES), jnp.int32),
            pltpu.VMEM((SUBLANES, LANES), jnp.int32),
            pltpu.VMEM((row_total, SUBLANES, LANES), jnp.float32),
            pltpu.VMEM((row_total, 3, SUBLANES, LANES), jnp.float32),
            pltpu.VMEM((SUBLANES, LANES), jnp.int32),
            pltpu.VMEM((3, 3, SUBLANES, LANES), jnp.int32),
            by_rows,
            by_rows,
            pltpu.VMEM((3, events, pieces, padded_rows, LANES), jnp.float32),
            state,
            state,
            state,
            pltpu.VMEM((fixed_tiles, 4, SUBLANES, width), jnp.float32),
            pltpu.SemaphoreType.DMA((len(small),)),
            pltpu.SemaphoreType.DMA((3,)),
            pltpu.SemaphoreType.DMA((len(REGIONS), 3)),
            pltpu.SemaphoreType.DMA((len(REGIONS), 3)),
            pltpu.SemaphoreType.DMA((row_total, 3)),
            pltpu.SemaphoreType.DMA((row_total, 3)),
            pltpu.SemaphoreType.DMA((len(REGIONS),)),
            pltpu.SemaphoreType.DMA((len(REGIONS),)),
            pltpu.SemaphoreType.REGULAR,
        ],
        compiler_params=pltpu.CompilerParams(
            collective_id=0, has_side_effects=True, vmem_limit_bytes=VMEM_BYTES
        ),
        name="flood",
    )(*[pltpu.with_memory_space_constraint(x, pltpu.HBM) for x in (*small, hand, drain, manning)])
    return start * (1.0 / SCALE), end * (1.0 / SCALE)


def solution(mesh):
    return jax.shard_map(
        functools.partial(body, mesh.shape["row"], mesh.shape["col"]),
        mesh=mesh,
        in_specs=(
            P("evt", ("grp", "row", "col")),
            P(("grp", "row"), "col", None, None),
            P(("grp", "row"), "col", None),
            P(("grp", "row"), "col", None),
            P(("grp", "row"), "col"),
            P(("grp", "row"), "col"),
            P(("grp", "row"), "col"),
            P(("grp", "row"), "col"),
        ),
        out_specs=(P("evt", ("grp", "row"), "col"), P("evt", ("grp", "row"), "col")),
        check_vma=False,
    )
```

```python
import functools

import jax
import jax.numpy as jnp
from jax import lax
from jax.experimental import pallas as pl
from jax.experimental.pallas import tpu as pltpu
from jax.sharding import PartitionSpec as P

STEPS = 16
GRAVITY = 9.81
TIMESTEP = 0.4
SPACING = 10.0
DEPTH_FLOOR = 0.05
DRY_SECTION = -1000.0

VMEM_BYTES = 24 * 1024 * 1024
LANES = 128
SUBLANES = 8
HALO = STEPS
SCALE = GRAVITY * TIMESTEP * TIMESTEP / (SPACING * SPACING)
DRAG_SCALE = (
    GRAVITY * TIMESTEP * SCALE ** (7.0 / 3.0) / (SCALE * TIMESTEP / SPACING)
)
REGIONS = tuple(
    (dr, dc) for dr in (-1, 0, 1) for dc in (-1, 0, 1) if (dr, dc) != (0, 0)
)
EDGE_STEPS = ((6, 7), (5, 9))
INNER_STEPS = ((8, 7), (6, 9))

TOGETHER_TILES = 6


def phases(has_north, has_south, own_tiles):
    if has_north and has_south:
        return [
            (-(tiles - own_tiles) * SUBLANES // 2, tiles, steps) for tiles, steps in INNER_STEPS
        ]
    return [
        (-(tiles - own_tiles) * SUBLANES if has_north else 0, tiles, steps)
        for tiles, steps in EDGE_STEPS
    ]


def row_spans(dr, tile_rows):
    if dr == -1:
        return pl.ds(tile_rows - HALO, HALO), pl.ds(0, HALO)
    if dr == 1:
        return pl.ds(0, HALO), pl.ds(HALO + tile_rows, HALO)
    return pl.ds(0, tile_rows), pl.ds(HALO, tile_rows)


def col_spans(dc, tile_cols):
    if dc == -1:
        return pl.ds(tile_cols - LANES, LANES), pl.ds(tile_cols + LANES, LANES)
    if dc == 1:
        return pl.ds(0, LANES), pl.ds(tile_cols, LANES)
    return pl.ds(0, tile_cols), pl.ds(0, tile_cols)


def pick_lanes(x, index):
    return jnp.take_along_axis(x, index, axis=1, mode="promise_in_bounds")


def flood_kernel(
    row_total, col_total,
    sections_in, send_list_in, send_count_in, slot_position_in, block_slot_in, hand, drain, manning,
    hand_depth, final_depth,
    sections, send_list, send_count, slot_position, block_slot,
    ext, lists, flat, slots, message, landed, place, where_held,
    bed_rows, drag_rows, rows, surface, east, south, fixed,
    small_sem, own_sem, strip_send, strip_recv, level_send, level_recv, place_send, place_recv, near_sem, far_sem,
):
    r = lax.axis_index("row")
    k = lax.axis_index("col")
    tile_rows, tile_cols = hand.shape
    events, catch_local = sections.shape
    capacity = send_list.shape[3]
    block_rows, block_cols = block_slot.shape
    blocks = block_rows * block_cols
    cols = tile_cols // LANES
    width = tile_cols + LANES
    own_tiles = tile_rows // SUBLANES
    halo_tiles = HALO // SUBLANES
    terrain = (hand, drain, manning)

    def row_exists(dr):
        return jnp.logical_and(r + dr >= 0, r + dr < row_total)

    def col_exists(dc):
        return jnp.logical_and(k + dc >= 0, k + dc < col_total)

    def tile_exists(dr, dc):
        if dr == 0:
            return col_exists(dc)
        if dc == 0:
            return row_exists(dr)
        return jnp.logical_and(row_exists(dr), col_exists(dc))

    def as_int(flag):
        return flag.astype(jnp.int32)

    earlier = ((-1, -1), (-1, 0), (-1, 1), (0, -1))
    later = ((1, -1), (1, 0), (1, 1), (0, 1))
    barrier = pltpu.get_barrier_semaphore()

    def is_earlier(rr, dc):
        there = (rr <= r) if dc == -1 else (rr < r)
        return there if dc == 0 else jnp.logical_and(there, col_exists(dc))

    def is_later(rr, dc):
        there = (rr >= r) if dc == 1 else (rr > r)
        return there if dc == 0 else jnp.logical_and(there, col_exists(dc))

    def is_near(rr, dc):
        return jnp.logical_and(rr - r <= 1, r - rr <= 1)

    partners = [(rr, dc) for rr in range(row_total) for dc in (-1, 0, 1)]

    def tell(semaphore, rr, dc):
        pl.semaphore_signal(
            semaphore, inc=1, device_id={"row": rr, "col": k + dc},
            device_id_type=pl.DeviceIdType.MESH,
        )

    for rr, dc in partners:
        @pl.when(is_later(rr, dc))
        def _():
            tell(barrier, rr, dc)

    small_copies = [
        pltpu.make_async_copy(source, target, small_sem.at[at])
        for at, (source, target) in enumerate((
            (sections_in, sections), (send_list_in, send_list), (send_count_in, send_count),
            (slot_position_in, slot_position), (block_slot_in, block_slot),
        ))
    ]
    own_copies = [
        pltpu.make_async_copy(
            terrain[array], ext.at[array, pl.ds(HALO, tile_rows), pl.ds(0, tile_cols)],
            own_sem.at[array],
        )
        for array in range(3)
    ]
    for copy in small_copies + own_copies:
        copy.start()

    ahead = sum(as_int(is_earlier(rr, dc)) for rr, dc in partners)

    @pl.when(ahead > 0)
    def _():
        pl.semaphore_wait(barrier, ahead)

    for rr, dc in partners:
        @pl.when(jnp.logical_and(is_earlier(rr, dc), is_near(rr, dc)))
        def _():
            tell(near_sem, rr, dc)

        @pl.when(jnp.logical_and(is_earlier(rr, dc), jnp.logical_not(is_near(rr, dc))))
        def _():
            tell(far_sem, rr, dc)

    lane = lax.broadcasted_iota(jnp.int32, (SUBLANES, LANES), 1)
    row_id = lax.broadcasted_iota(jnp.int32, (SUBLANES, LANES), 0)
    near = lane < LANES // 2
    lists[...] = jnp.zeros(lists.shape, jnp.int32)
    flat[...] = jnp.zeros(flat.shape, jnp.int32)
    slots[...] = jnp.zeros(slots.shape, jnp.int32)
    for copy in small_copies:
        copy.wait()

    lane_of = lax.broadcasted_iota(jnp.int32, (1, capacity), 1)
    for rr in range(row_total):
        live = lane_of < jnp.broadcast_to(send_count[0, :, rr : rr + 1], (1, capacity))
        held = jnp.where(live, send_list[0, 0, rr : rr + 1, :], -1)
        for e in range(events):
            lists[rr : rr + 1, e * capacity : (e + 1) * capacity] = held
    list_rows = lists.shape[0]
    lane_tall = lax.broadcasted_iota(jnp.int32, (list_rows, LANES), 1)
    wanted = lists[...]
    local = jnp.maximum(wanted, 0)
    values = jnp.full((list_rows, LANES), DRY_SECTION, jnp.float32)
    for half in range(catch_local // LANES):
        mine = jnp.logical_and(wanted >= half * LANES, wanted < (half + 1) * LANES)
        for e in range(events):
            source = jnp.broadcast_to(
                sections[e : e + 1, half * LANES : (half + 1) * LANES], (list_rows, LANES)
            )
            found = pick_lanes(source, jnp.bitwise_and(local, LANES - 1))
            of_event = jnp.logical_and(lane_tall >= e * capacity, lane_tall < (e + 1) * capacity)
            values = jnp.where(jnp.logical_and(mine, of_event), found, values)
    for rr in range(row_total):
        message[rr] = jnp.full((SUBLANES, LANES), DRY_SECTION, jnp.float32)
        for j in (-1, 0, 1):
            pick = min(max(rr + j, 0), row_total - 1)
            message[rr, j + 1 : j + 2, :] = values[pick : pick + 1, :]

    def level_copy(rr, dc, arriving):
        at = (rr, 1 + dc) if arriving else (r, 1 - dc)
        return pltpu.make_async_remote_copy(
            src_ref=message.at[rr],
            dst_ref=landed.at[at],
            send_sem=level_send.at[rr, dc + 1],
            recv_sem=level_recv.at[at],
            device_id={"row": rr, "col": k + dc},
            device_id_type=pl.DeviceIdType.MESH,
        )

    def place_copy(index, dr, dc):
        return pltpu.make_async_remote_copy(
            src_ref=place,
            dst_ref=where_held.at[1 + dr, 1 + dc],
            send_sem=place_send.at[index],
            recv_sem=place_recv.at[index],
            device_id={"row": r - dr, "col": k - dc},
            device_id_type=pl.DeviceIdType.MESH,
        )

    def strip_copy(index, array, dr, dc):
        src_rows, dst_rows = row_spans(dr, tile_rows)
        src_cols, dst_cols = col_spans(dc, tile_cols)
        return pltpu.make_async_remote_copy(
            src_ref=terrain[array].at[src_rows, src_cols],
            dst_ref=ext.at[array, dst_rows, dst_cols],
            send_sem=strip_send.at[index, array],
            recv_sem=strip_recv.at[index, array],
            device_id={"row": r - dr, "col": k - dc},
            device_id_type=pl.DeviceIdType.MESH,
        )

    def send_levels(chosen):
        for rr, dc in partners:
            @pl.when(chosen(rr, dc))
            def _():
                level_copy(rr, dc, False).start()

    def send_near(targets):
        for index, (dr, dc) in enumerate(REGIONS):
            if (-dr, -dc) in targets:
                @pl.when(tile_exists(-dr, -dc))
                def _():
                    place_copy(index, dr, dc).start()
                    for array in range(3):
                        strip_copy(index, array, dr, dc).start()

    send_levels(is_earlier)

    slots[0:1, 0 : slot_position.shape[2]] = slot_position[0]
    for e in range(events):
        for row in range(block_rows):
            at = e * blocks + row * block_cols
            flat[0:1, at : at + block_cols] = block_slot[row : row + 1, :]
    tile_shape = (SUBLANES, LANES)
    own_place = pick_lanes(
        jnp.broadcast_to(slots[0:1, :], tile_shape), jnp.broadcast_to(flat[0:1, :], tile_shape)
    )
    place[...] = own_place
    where_held[1, 1] = own_place

    send_near(earlier)
    behind = sum(as_int(tile_exists(dr, dc)) for dr, dc in later)
    beyond = sum(as_int(is_later(rr, dc)) for rr, dc in partners) - behind

    @pl.when(behind > 0)
    def _():
        pl.semaphore_wait(near_sem, behind)

    send_near(later)

    @pl.when(beyond > 0)
    def _():
        pl.semaphore_wait(far_sem, beyond)

    send_levels(is_later)
    landed[r, 1] = message[r]

    lane_ok = jnp.where(near, as_int(col_exists(1)), as_int(col_exists(-1))) > 0
    wide_row = lax.broadcasted_iota(jnp.int32, (SUBLANES, width), 0)
    last_row = wide_row == SUBLANES - 1
    first_row = wide_row == 0

    def span(t):
        return pl.ds(t * SUBLANES, SUBLANES)

    def piece(j):
        return slice(j * LANES, (j + 1) * LANES)

    def up(x):
        return pltpu.roll(x, SUBLANES - 1, 0)

    def down(x):
        return pltpu.roll(x, 1, 0)

    def left(x):
        return pltpu.roll(x, width - 1, 1)

    def right(x):
        return pltpu.roll(x, 1, 1)

    def guard(x):
        return jnp.concatenate(
            [x[:, :tile_cols], jnp.where(lane_ok, x[:, tile_cols:], 0.0)], 1
        )

    def beside(array, t):
        return jnp.where(
            near,
            ext[array, span(t), tile_cols : tile_cols + LANES],
            ext[array, span(t), tile_cols + LANES : tile_cols + 2 * LANES],
        )

    def set_terrain(t, side):
        if side:
            height, low, rough = [beside(array, t) for array in range(3)]
            bed_rows[cols, span(t), :] = jnp.where(lane_ok, SCALE * (height + low), 0.0)
            drag_rows[cols, span(t), :] = jnp.where(lane_ok, DRAG_SCALE * (rough * rough), 0.0)
            return
        for j in range(cols):
            height, low, rough = [ext[array, span(t), piece(j)] for array in range(3)]
            bed_rows[j, span(t), :] = SCALE * (height + low)
            drag_rows[j, span(t), :] = DRAG_SCALE * (rough * rough)

    def spread(ref, first, tiles, t):
        return jnp.concatenate(
            [ref[j, pl.ds(first + t, SUBLANES, stride=tiles), :] for j in range(cols + 1)], 1
        )

    def gather_back(ref, first, tiles, t, x):
        for j in range(cols + 1):
            ref[j, pl.ds(first + t, SUBLANES, stride=tiles), :] = x[:, piece(j)]

    def level_of(held, dr, lane_at):
        return jnp.broadcast_to(held[dr + 1 : dr + 2, lane_at : lane_at + 1], tile_shape)

    def face(flow, here, beyond, top, rough):
        thick = jnp.maximum(here, beyond) - top
        power = jnp.exp2((-7.0 / 3.0) * jnp.log2(jnp.maximum(thick, SCALE * DEPTH_FLOOR)))
        pushed = flow - thick * (beyond - here)
        return pushed * pl.reciprocal(1.0 + rough * jnp.abs(flow) * power, approx=True)

    def flood(has_north, has_south):
        plan = [(first + HALO, tiles, steps) for first, tiles, steps in phases(has_north, has_south, own_tiles)]
        row_tiles = range(
            0 if has_north else halo_tiles,
            halo_tiles + own_tiles + (halo_tiles if has_south else 0),
        )

        def below(bottom, x):
            x = up(x)
            return x if has_south else jnp.where(last_row, 0.0, x)

        for t in range(halo_tiles, halo_tiles + own_tiles):
            set_terrain(t, False)
        for index, (dr, dc) in enumerate(REGIONS):
            if (dr == -1 and not has_north) or (dr == 1 and not has_south):
                continue

            @pl.when(col_exists(dc))
            def _():
                for array in range(3):
                    strip_copy(index, array, dr, dc).wait_recv()
        for t in row_tiles:
            if t < halo_tiles or t >= halo_tiles + own_tiles:
                set_terrain(t, False)
            set_terrain(t, True)

        base = 0
        for first, tiles, _ in plan:
            start = spread(bed_rows, first, tiles, 0)
            here = start
            for t in range(tiles):
                after = below(True, start) if t == tiles - 1 else spread(bed_rows, first, tiles, t + 1)
                fixed[base + t, 0] = here
                fixed[base + t, 1] = jnp.maximum(here, left(here))
                fixed[base + t, 2] = jnp.maximum(here, after)
                fixed[base + t, 3] = spread(drag_rows, first, tiles, t)
                here = after
            base += tiles
        for t in range(plan[0][1]):
            for e in range(events):
                east[e, t] = jnp.zeros((SUBLANES, width), jnp.float32)
                south[e, t] = jnp.zeros((SUBLANES, width), jnp.float32)

        for index, (dr, dc) in enumerate(REGIONS):
            if (dr == -1 and not has_north) or (dr == 1 and not has_south):
                continue

            @pl.when(col_exists(dc))
            def _():
                place_copy(index, dr, dc).wait_recv()
        for rr in range(row_total):
            for dc in (-1, 0, 1):
                there = (rr != r) if dc == 0 else col_exists(dc)

                @pl.when(there)
                def _():
                    level_copy(rr, dc, True).wait_recv()

        event_shift = jnp.where(lane >= blocks, capacity, 0)
        levels = []
        for kc in range(3):
            placed = jnp.where(
                row_id == 0, where_held[0, kc], jnp.where(row_id == 1, where_held[1, kc], where_held[2, kc])
            )
            source = lax.shift_right_logical(placed, capacity.bit_length() - 1)
            at = jnp.bitwise_and(placed, capacity - 1) + event_shift
            level = jnp.full(tile_shape, DRY_SECTION, jnp.float32)
            for rr in range(row_total):
                level = jnp.where(source == rr, pick_lanes(landed[rr, kc], at), level)
            levels.append(level)

        for t in row_tiles:
            dr, row = 0, t - halo_tiles
            if t < halo_tiles:
                dr, row = -1, block_rows - halo_tiles + t
            elif row >= own_tiles:
                dr, row = 1, row - own_tiles
            side_height = beside(0, t)
            for e in range(events):
                at = e * blocks + row * block_cols
                for j in range(cols):
                    value = SCALE * jnp.maximum(
                        level_of(levels[1], dr, at + j) - ext[0, span(t), piece(j)], 0.0
                    )
                    if dr == 0:
                        hand_depth[e, span(row), piece(j)] = value
                    rows[0, e, j, span(t), :] = value + bed_rows[j, span(t), :]
                level = jnp.where(
                    near, level_of(levels[2], dr, at), level_of(levels[0], dr, at + block_cols - 1)
                )
                value = SCALE * jnp.maximum(level - side_height, 0.0) + bed_rows[cols, span(t), :]
                rows[0, e, cols, span(t), :] = jnp.where(lane_ok, value, 0.0)

        def one_step(base, tiles, chosen):
            end = tiles - 1
            for e in chosen:
                def go_south(t, here, beyond):
                    return face(south[e, t], here, beyond, fixed[base + t, 2], fixed[base + t, 3])

                start = surface[e, 0]
                final_south = go_south(end, surface[e, end], below(True, start))
                above = down(final_south)
                if not has_north:
                    above = jnp.where(first_row, (fixed[base, 0] - start) * start, above)
                here = start
                for t in range(tiles):
                    if t == end:
                        new_south = final_south
                        after = None
                    else:
                        after = surface[e, t + 1]
                        new_south = go_south(t, here, after)
                    new_east = face(
                        east[e, t], here, left(here), fixed[base + t, 1], fixed[base + t, 3]
                    )
                    change = (right(new_east) - new_east) + (above - new_south)
                    surface[e, t] = guard(jnp.maximum(here + change, fixed[base + t, 0]))
                    east[e, t] = guard(new_east)
                    south[e, t] = new_south
                    above = new_south
                    here = after

        base = 0
        for number, (first, tiles, steps) in enumerate(plan):
            if number > 0:
                old_first, old_tiles, _ = plan[number - 1]
                for e in range(events):
                    for which, ref in enumerate((surface, east, south)):
                        for t in range(old_tiles):
                            gather_back(rows.at[which, e], old_first, old_tiles, t, ref[e, t])
            for e in range(events):
                for which, ref in enumerate((surface, east, south)):
                    if number > 0 or which == 0:
                        for t in range(tiles):
                            ref[e, t] = spread(rows.at[which, e], first, tiles, t)

            def one(turn, carry, base=base, tiles=tiles):
                one_step(base, tiles, range(events))
                return carry

            def one_apart(turn, carry, base=base, tiles=tiles):
                one_step(base, tiles, (lax.rem(turn, events),))
                return carry

            if tiles <= TOGETHER_TILES:
                lax.fori_loop(0, steps, one, 0)
            else:
                lax.fori_loop(0, steps * events, one_apart, 0)
            base += tiles
        first, tiles, _ = plan[-1]
        for e in range(events):
            for t in range(tiles):
                gather_back(rows.at[0, e], first, tiles, t, surface[e, t])
            for t in range(own_tiles):
                for j in range(cols):
                    at = span(halo_tiles + t)
                    final_depth[e, span(t), piece(j)] = rows[0, e, j, at, :] - bed_rows[j, at, :]

    for copy in own_copies:
        copy.wait()

    @pl.when(r == 0)
    def _():
        flood(False, True)

    @pl.when(jnp.logical_and(r > 0, r < row_total - 1))
    def _():
        flood(True, True)

    @pl.when(r == row_total - 1)
    def _():
        flood(True, False)

    for index, (dr, dc) in enumerate(REGIONS):
        @pl.when(tile_exists(-dr, -dc))
        def _():
            place_copy(index, dr, dc).wait_send()
            for array in range(3):
                strip_copy(index, array, dr, dc).wait_send()
    for rr in range(row_total):
        for dc in (-1, 0, 1):
            there = (rr != r) if dc == 0 else col_exists(dc)

            @pl.when(there)
            def _():
                level_copy(rr, dc, False).wait_send()


def body(
    row_total, col_total,
    sections, send_list, send_count, slot_sender_position, block_slot_index, hand, drain, manning,
):
    events = sections.shape[0]
    tile_rows, tile_cols = hand.shape
    vmem = pl.BlockSpec(memory_space=pltpu.VMEM)
    hbm = pl.BlockSpec(memory_space=pltpu.HBM)
    padded_rows = tile_rows + 2 * HALO
    padded_tiles = padded_rows // SUBLANES
    width = tile_cols + LANES
    pieces = width // LANES
    small = (sections, send_list, send_count, slot_sender_position, block_slot_index)
    list_rows = -(-row_total // SUBLANES) * SUBLANES
    fixed_tiles = max(
        sum(tiles for tiles, _ in EDGE_STEPS), sum(tiles for tiles, _ in INNER_STEPS)
    )
    by_rows = pltpu.VMEM((pieces, padded_rows, LANES), jnp.float32)
    state = pltpu.VMEM((events, padded_tiles, SUBLANES, width), jnp.float32)
    out = jax.ShapeDtypeStruct((events, tile_rows, tile_cols), jnp.float32)
    start, end = pl.pallas_call(
        functools.partial(flood_kernel, row_total, col_total),
        out_shape=(out, out),
        in_specs=[hbm] * 8,
        out_specs=(vmem, vmem),
        scratch_shapes=[pltpu.VMEM(x.shape, x.dtype) for x in small]
        + [
            pltpu.VMEM((3, padded_rows, tile_cols + 2 * LANES), jnp.float32),
            pltpu.VMEM((list_rows, LANES), jnp.int32),
            pltpu.VMEM((SUBLANES, LANES), jnp.int32),
            pltpu.VMEM((SUBLANES, LANES), jnp.int32),
            pltpu.VMEM((row_total, SUBLANES, LANES), jnp.float32),
            pltpu.VMEM((row_total, 3, SUBLANES, LANES), jnp.float32),
            pltpu.VMEM((SUBLANES, LANES), jnp.int32),
            pltpu.VMEM((3, 3, SUBLANES, LANES), jnp.int32),
            by_rows,
            by_rows,
            pltpu.VMEM((3, events, pieces, padded_rows, LANES), jnp.float32),
            state,
            state,
            state,
            pltpu.VMEM((fixed_tiles, 4, SUBLANES, width), jnp.float32),
            pltpu.SemaphoreType.DMA((len(small),)),
            pltpu.SemaphoreType.DMA((3,)),
            pltpu.SemaphoreType.DMA((len(REGIONS), 3)),
            pltpu.SemaphoreType.DMA((len(REGIONS), 3)),
            pltpu.SemaphoreType.DMA((row_total, 3)),
            pltpu.SemaphoreType.DMA((row_total, 3)),
            pltpu.SemaphoreType.DMA((len(REGIONS),)),
            pltpu.SemaphoreType.DMA((len(REGIONS),)),
            pltpu.SemaphoreType.REGULAR,
            pltpu.SemaphoreType.REGULAR,
        ],
        compiler_params=pltpu.CompilerParams(
            collective_id=0, has_side_effects=True, vmem_limit_bytes=VMEM_BYTES
        ),
        name="flood",
    )(*[pltpu.with_memory_space_constraint(x, pltpu.HBM) for x in (*small, hand, drain, manning)])
    return start * (1.0 / SCALE), end * (1.0 / SCALE)


def solution(mesh):
    return jax.shard_map(
        functools.partial(body, mesh.shape["row"], mesh.shape["col"]),
        mesh=mesh,
        in_specs=(
            P("evt", ("grp", "row", "col")),
            P(("grp", "row"), "col", None, None),
            P(("grp", "row"), "col", None),
            P(("grp", "row"), "col", None),
            P(("grp", "row"), "col"),
            P(("grp", "row"), "col"),
            P(("grp", "row"), "col"),
            P(("grp", "row"), "col"),
        ),
        out_specs=(P("evt", ("grp", "row"), "col"), P("evt", ("grp", "row"), "col")),
        check_vma=False,
    )
```

```python
import functools

import jax
import jax.numpy as jnp
from jax import lax
from jax.experimental import pallas as pl
from jax.experimental.pallas import tpu as pltpu
from jax.sharding import PartitionSpec as P

STEPS = 16
GRAVITY = 9.81
TIMESTEP = 0.4
SPACING = 10.0
DEPTH_FLOOR = 0.05
DRY_SECTION = -1000.0

VMEM_BYTES = 24 * 1024 * 1024
LANES = 128
SUBLANES = 8
HALO = STEPS
SCALE = GRAVITY * TIMESTEP * TIMESTEP / (SPACING * SPACING)
DRAG_SCALE = (
    GRAVITY * TIMESTEP * SCALE ** (7.0 / 3.0) / (SCALE * TIMESTEP / SPACING)
)
REGIONS = tuple(
    (dr, dc) for dr in (-1, 0, 1) for dc in (-1, 0, 1) if (dr, dc) != (0, 0)
)
EDGE_STEPS = ((6, 7), (5, 9))
INNER_STEPS = ((8, 3), (7, 4), (6, 4), (5, 5))

TOGETHER_TILES = 6


def phases(has_north, has_south, own_tiles):
    if has_north and has_south:
        return [
            (-(tiles - own_tiles) * SUBLANES // 2, tiles, steps) for tiles, steps in INNER_STEPS
        ]
    return [
        (-(tiles - own_tiles) * SUBLANES if has_north else 0, tiles, steps)
        for tiles, steps in EDGE_STEPS
    ]


def row_spans(dr, tile_rows):
    if dr == -1:
        return pl.ds(tile_rows - HALO, HALO), pl.ds(0, HALO)
    if dr == 1:
        return pl.ds(0, HALO), pl.ds(HALO + tile_rows, HALO)
    return pl.ds(0, tile_rows), pl.ds(HALO, tile_rows)


def col_spans(dc, tile_cols):
    if dc == -1:
        return pl.ds(tile_cols - LANES, LANES), pl.ds(tile_cols + LANES, LANES)
    if dc == 1:
        return pl.ds(0, LANES), pl.ds(tile_cols, LANES)
    return pl.ds(0, tile_cols), pl.ds(0, tile_cols)


def pick_lanes(x, index):
    return jnp.take_along_axis(x, index, axis=1, mode="promise_in_bounds")


def flood_kernel(
    row_total, col_total, cores,
    sections_in, send_list_in, send_count_in, slot_position_in, block_slot_in, hand, drain, manning,
    hand_depth, final_depth,
    sections, send_list, send_count, slot_position, block_slot,
    ext, lists, flat, slots, message, landed, place, where_held,
    bed_rows, drag_rows, rows, surface, east, south, fixed,
    small_sem, own_sem, strip_send, strip_recv, level_send, level_recv, place_send, place_recv, pass_send, pass_recv, near_sem, far_sem, sibling_sem,
):
    r = lax.axis_index("row")
    k = lax.axis_index("col")
    core = lax.axis_index("evt")
    tile_rows, tile_cols = hand.shape
    events, catch_local = sections.shape
    capacity = send_list.shape[3]
    block_rows, block_cols = block_slot.shape
    blocks = block_rows * block_cols
    cols = tile_cols // LANES
    width = tile_cols + LANES
    own_tiles = tile_rows // SUBLANES
    halo_tiles = HALO // SUBLANES
    terrain = (hand, drain, manning)
    shared = cores == 2
    share = tile_cols // 2 if shared else tile_cols
    tall = tuple((index, dr) for index, (dr, dc) in enumerate(REGIONS) if dc == 0)

    def row_exists(dr):
        return jnp.logical_and(r + dr >= 0, r + dr < row_total)

    def col_exists(dc):
        return jnp.logical_and(k + dc >= 0, k + dc < col_total)

    def tile_exists(dr, dc):
        if dr == 0:
            return col_exists(dc)
        if dc == 0:
            return row_exists(dr)
        return jnp.logical_and(row_exists(dr), col_exists(dc))

    def as_int(flag):
        return flag.astype(jnp.int32)

    earlier = ((-1, -1), (-1, 0), (-1, 1), (0, -1))
    later = ((1, -1), (1, 0), (1, 1), (0, 1))
    barrier = pltpu.get_barrier_semaphore()

    def is_earlier(rr, dc):
        there = (rr <= r) if dc == -1 else (rr < r)
        return there if dc == 0 else jnp.logical_and(there, col_exists(dc))

    def is_later(rr, dc):
        there = (rr >= r) if dc == 1 else (rr > r)
        return there if dc == 0 else jnp.logical_and(there, col_exists(dc))

    def is_near(rr, dc):
        return jnp.logical_and(rr - r <= 1, r - rr <= 1)

    partners = [(rr, dc) for rr in range(row_total) for dc in (-1, 0, 1)]

    def tell(semaphore, rr, dc):
        pl.semaphore_signal(
            semaphore, inc=1, device_id={"row": rr, "col": k + dc},
            device_id_type=pl.DeviceIdType.MESH,
        )

    for rr, dc in partners:
        @pl.when(is_later(rr, dc))
        def _():
            tell(barrier, rr, dc)

    def tell_sibling(semaphore):
        pl.semaphore_signal(
            semaphore, inc=1, device_id={"evt": 1 - core}, device_id_type=pl.DeviceIdType.MESH
        )

    if shared:
        @pl.when(core == 0)
        def _():
            tell_sibling(barrier)

    small_copies = [
        pltpu.make_async_copy(source, target, small_sem.at[at])
        for at, (source, target) in enumerate((
            (sections_in, sections), (send_list_in, send_list), (send_count_in, send_count),
            (slot_position_in, slot_position), (block_slot_in, block_slot),
        ))
    ]
    own_copies = [
        pltpu.make_async_copy(
            terrain[array], ext.at[array, pl.ds(HALO, tile_rows), pl.ds(0, tile_cols)],
            own_sem.at[array],
        )
        for array in range(3)
    ]
    for copy in small_copies + own_copies:
        copy.start()

    ahead = sum(as_int(is_earlier(rr, dc)) for rr, dc in partners)
    if shared:
        ahead = ahead + as_int(core == 1)

    @pl.when(ahead > 0)
    def _():
        pl.semaphore_wait(barrier, ahead)

    if shared:
        @pl.when(core == 1)
        def _():
            tell_sibling(sibling_sem)

    for rr, dc in partners:
        @pl.when(jnp.logical_and(is_earlier(rr, dc), is_near(rr, dc)))
        def _():
            tell(near_sem, rr, dc)

        @pl.when(jnp.logical_and(is_earlier(rr, dc), jnp.logical_not(is_near(rr, dc))))
        def _():
            tell(far_sem.at[r], rr, dc)

    def strip_copy(index, array, dr, dc):
        src_rows, dst_rows = row_spans(dr, tile_rows)
        src_cols, dst_cols = col_spans(dc, tile_cols)
        if dc == 0:
            src_cols = dst_cols = pl.ds(pl.multiple_of(core * share, LANES) if shared else 0, share)
        return pltpu.make_async_remote_copy(
            src_ref=terrain[array].at[src_rows, src_cols],
            dst_ref=ext.at[array, dst_rows, dst_cols],
            send_sem=strip_send.at[index, array],
            recv_sem=strip_recv.at[index, array],
            device_id={"row": r - dr, "col": k - dc},
            device_id_type=pl.DeviceIdType.MESH,
        )

    def pass_on(index, array, dr):
        held = ext.at[
            array, row_spans(dr, tile_rows)[1], pl.ds(pl.multiple_of(core * share, LANES), share)
        ]
        return pltpu.make_async_remote_copy(
            src_ref=held,
            dst_ref=held,
            send_sem=pass_send.at[index, array],
            recv_sem=pass_recv.at[index, array],
            device_id={"evt": 1 - core},
            device_id_type=pl.DeviceIdType.MESH,
        )

    def send_strips(targets):
        for index, (dr, dc) in enumerate(REGIONS):
            if (-dr, -dc) in targets:
                @pl.when(tile_exists(-dr, -dc))
                def _():
                    for array in range(3):
                        strip_copy(index, array, dr, dc).start()

    @pl.when(r < row_total - 1)
    def _():
        send_strips(earlier)

    lane = lax.broadcasted_iota(jnp.int32, (SUBLANES, LANES), 1)
    row_id = lax.broadcasted_iota(jnp.int32, (SUBLANES, LANES), 0)
    near = lane < LANES // 2
    lists[...] = jnp.zeros(lists.shape, jnp.int32)
    flat[...] = jnp.zeros(flat.shape, jnp.int32)
    slots[...] = jnp.zeros(slots.shape, jnp.int32)
    for copy in small_copies:
        copy.wait()

    lane_of = lax.broadcasted_iota(jnp.int32, (1, capacity), 1)
    for rr in range(row_total):
        live = lane_of < jnp.broadcast_to(send_count[0, :, rr : rr + 1], (1, capacity))
        held = jnp.where(live, send_list[0, 0, rr : rr + 1, :], -1)
        for e in range(events):
            lists[rr : rr + 1, e * capacity : (e + 1) * capacity] = held
    list_rows = lists.shape[0]
    lane_tall = lax.broadcasted_iota(jnp.int32, (list_rows, LANES), 1)
    wanted = lists[...]
    local = jnp.maximum(wanted, 0)
    values = jnp.full((list_rows, LANES), DRY_SECTION, jnp.float32)
    for half in range(catch_local // LANES):
        mine = jnp.logical_and(wanted >= half * LANES, wanted < (half + 1) * LANES)
        for e in range(events):
            source = jnp.broadcast_to(
                sections[e : e + 1, half * LANES : (half + 1) * LANES], (list_rows, LANES)
            )
            found = pick_lanes(source, jnp.bitwise_and(local, LANES - 1))
            of_event = jnp.logical_and(lane_tall >= e * capacity, lane_tall < (e + 1) * capacity)
            values = jnp.where(jnp.logical_and(mine, of_event), found, values)
    for rr in range(row_total):
        message[rr] = jnp.full((SUBLANES, LANES), DRY_SECTION, jnp.float32)
        for j in (-1, 0, 1):
            pick = min(max(rr + j, 0), row_total - 1)
            message[rr, j + 1 : j + 2, :] = values[pick : pick + 1, :]

    def level_copy(rr, dc, arriving):
        at = (rr, 1 + dc) if arriving else (r, 1 - dc)
        return pltpu.make_async_remote_copy(
            src_ref=message.at[rr],
            dst_ref=landed.at[at],
            send_sem=level_send.at[rr, dc + 1],
            recv_sem=level_recv.at[at],
            device_id={"row": rr, "col": k + dc},
            device_id_type=pl.DeviceIdType.MESH,
        )

    def place_copy(index, dr, dc):
        return pltpu.make_async_remote_copy(
            src_ref=place,
            dst_ref=where_held.at[1 + dr, 1 + dc],
            send_sem=place_send.at[index],
            recv_sem=place_recv.at[index],
            device_id={"row": r - dr, "col": k - dc},
            device_id_type=pl.DeviceIdType.MESH,
        )

    def send_levels(chosen):
        for rr, dc in partners:
            @pl.when(chosen(rr, dc))
            def _():
                level_copy(rr, dc, False).start()

    def send_place(targets):
        for index, (dr, dc) in enumerate(REGIONS):
            if (-dr, -dc) in targets:
                @pl.when(tile_exists(-dr, -dc))
                def _():
                    place_copy(index, dr, dc).start()

    send_levels(is_earlier)

    slots[0:1, 0 : slot_position.shape[2]] = slot_position[0]
    for e in range(events):
        for row in range(block_rows):
            at = e * blocks + row * block_cols
            flat[0:1, at : at + block_cols] = block_slot[row : row + 1, :]
    tile_shape = (SUBLANES, LANES)
    own_place = pick_lanes(
        jnp.broadcast_to(slots[0:1, :], tile_shape), jnp.broadcast_to(flat[0:1, :], tile_shape)
    )
    place[...] = own_place
    where_held[1, 1] = own_place

    send_place(earlier)

    @pl.when(r == row_total - 1)
    def _():
        send_strips(earlier)

    behind = sum(as_int(tile_exists(dr, dc)) for dr, dc in later)

    @pl.when(behind > 0)
    def _():
        pl.semaphore_wait(near_sem, behind)

    send_levels(lambda rr, dc: jnp.logical_and(is_later(rr, dc), is_near(rr, dc)))
    send_strips(later)
    send_place(later)
    reach = sum(as_int(col_exists(dc)) for dc in (-1, 0, 1))
    for row in range(row_total):
        @pl.when(row > r + 1)
        def _():
            pl.semaphore_wait(far_sem.at[row], reach)

            for rr, dc in partners:
                if rr == row:
                    @pl.when(is_later(rr, dc))
                    def _():
                        level_copy(rr, dc, False).start()

    landed[r, 1] = message[r]

    lane_ok = jnp.where(near, as_int(col_exists(1)), as_int(col_exists(-1))) > 0
    wide_row = lax.broadcasted_iota(jnp.int32, (SUBLANES, width), 0)
    last_row = wide_row == SUBLANES - 1
    first_row = wide_row == 0

    def span(t):
        return pl.ds(t * SUBLANES, SUBLANES)

    def piece(j):
        return slice(j * LANES, (j + 1) * LANES)

    def up(x):
        return pltpu.roll(x, SUBLANES - 1, 0)

    def down(x):
        return pltpu.roll(x, 1, 0)

    def left(x):
        return pltpu.roll(x, width - 1, 1)

    def right(x):
        return pltpu.roll(x, 1, 1)

    def guard(x):
        return jnp.concatenate(
            [x[:, :tile_cols], jnp.where(lane_ok, x[:, tile_cols:], 0.0)], 1
        )

    def beside(array, t):
        return jnp.where(
            near,
            ext[array, span(t), tile_cols : tile_cols + LANES],
            ext[array, span(t), tile_cols + LANES : tile_cols + 2 * LANES],
        )

    def set_terrain(t, side):
        if side:
            height, low, rough = [beside(array, t) for array in range(3)]
            bed_rows[cols, span(t), :] = jnp.where(lane_ok, SCALE * (height + low), 0.0)
            drag_rows[cols, span(t), :] = jnp.where(lane_ok, DRAG_SCALE * (rough * rough), 0.0)
            return
        for j in range(cols):
            height, low, rough = [ext[array, span(t), piece(j)] for array in range(3)]
            bed_rows[j, span(t), :] = SCALE * (height + low)
            drag_rows[j, span(t), :] = DRAG_SCALE * (rough * rough)

    def spread(ref, first, tiles, t):
        return jnp.concatenate(
            [ref[j, pl.ds(first + t, SUBLANES, stride=tiles), :] for j in range(cols + 1)], 1
        )

    def gather_back(ref, first, tiles, t, x):
        for j in range(cols + 1):
            ref[j, pl.ds(first + t, SUBLANES, stride=tiles), :] = x[:, piece(j)]

    def level_of(held, dr, lane_at):
        return jnp.broadcast_to(held[dr + 1 : dr + 2, lane_at : lane_at + 1], tile_shape)

    def face(flow, here, beyond, top, rough):
        thick = jnp.maximum(here, beyond) - top
        power = jnp.exp2((-7.0 / 3.0) * jnp.log2(jnp.maximum(thick, SCALE * DEPTH_FLOOR)))
        pushed = flow - thick * (beyond - here)
        return pushed * pl.reciprocal(1.0 + rough * jnp.abs(flow) * power, approx=True)

    def flood(has_north, has_south):
        plan = [(first + HALO, tiles, steps) for first, tiles, steps in phases(has_north, has_south, own_tiles)]
        row_tiles = range(
            0 if has_north else halo_tiles,
            halo_tiles + own_tiles + (halo_tiles if has_south else 0),
        )

        def below(bottom, x):
            x = up(x)
            return x if has_south else jnp.where(last_row, 0.0, x)

        for t in range(halo_tiles, halo_tiles + own_tiles):
            set_terrain(t, False)
        halos = [(index, dr) for index, dr in tall if (has_north if dr == -1 else has_south)]
        if shared:
            @pl.when(core == 0)
            def _():
                pl.semaphore_wait(sibling_sem, 1)

        for array in range(3):
            for index, dr in halos:
                strip_copy(index, array, dr, 0).wait_recv()
                if shared:
                    pass_on(index, array, dr).start()
        for index, (dr, dc) in enumerate(REGIONS):
            if dc == 0 or (dr == -1 and not has_north) or (dr == 1 and not has_south):
                continue

            @pl.when(col_exists(dc))
            def _():
                for array in range(3):
                    strip_copy(index, array, dr, dc).wait_recv()
        for t in row_tiles:
            set_terrain(t, True)
        if shared:
            for array in range(3):
                for index, dr in halos:
                    pass_on(index, array, dr).wait_recv()
        for t in row_tiles:
            if t < halo_tiles or t >= halo_tiles + own_tiles:
                set_terrain(t, False)

        base = 0
        for first, tiles, _ in plan:
            start = spread(bed_rows, first, tiles, 0)
            here = start
            for t in range(tiles):
                after = below(True, start) if t == tiles - 1 else spread(bed_rows, first, tiles, t + 1)
                fixed[base + t, 0] = here
                fixed[base + t, 1] = jnp.maximum(here, left(here))
                fixed[base + t, 2] = jnp.maximum(here, after)
                fixed[base + t, 3] = spread(drag_rows, first, tiles, t)
                here = after
            base += tiles
        for t in range(plan[0][1]):
            for e in range(events):
                east[e, t] = jnp.zeros((SUBLANES, width), jnp.float32)
                south[e, t] = jnp.zeros((SUBLANES, width), jnp.float32)

        for index, (dr, dc) in enumerate(REGIONS):
            if (dr == -1 and not has_north) or (dr == 1 and not has_south):
                continue

            @pl.when(col_exists(dc))
            def _():
                place_copy(index, dr, dc).wait_recv()
        for rr in range(row_total):
            for dc in (-1, 0, 1):
                there = (rr != r) if dc == 0 else col_exists(dc)

                @pl.when(there)
                def _():
                    level_copy(rr, dc, True).wait_recv()

        event_shift = jnp.where(lane >= blocks, capacity, 0)
        levels = []
        for kc in range(3):
            placed = jnp.where(
                row_id == 0, where_held[0, kc], jnp.where(row_id == 1, where_held[1, kc], where_held[2, kc])
            )
            source = lax.shift_right_logical(placed, capacity.bit_length() - 1)
            at = jnp.bitwise_and(placed, capacity - 1) + event_shift
            level = jnp.full(tile_shape, DRY_SECTION, jnp.float32)
            for rr in range(row_total):
                level = jnp.where(source == rr, pick_lanes(landed[rr, kc], at), level)
            levels.append(level)

        for t in row_tiles:
            dr, row = 0, t - halo_tiles
            if t < halo_tiles:
                dr, row = -1, block_rows - halo_tiles + t
            elif row >= own_tiles:
                dr, row = 1, row - own_tiles
            side_height = beside(0, t)
            for e in range(events):
                at = e * blocks + row * block_cols
                for j in range(cols):
                    value = SCALE * jnp.maximum(
                        level_of(levels[1], dr, at + j) - ext[0, span(t), piece(j)], 0.0
                    )
                    if dr == 0:
                        hand_depth[e, span(row), piece(j)] = value
                    rows[0, e, j, span(t), :] = value + bed_rows[j, span(t), :]
                level = jnp.where(
                    near, level_of(levels[2], dr, at), level_of(levels[0], dr, at + block_cols - 1)
                )
                value = SCALE * jnp.maximum(level - side_height, 0.0) + bed_rows[cols, span(t), :]
                rows[0, e, cols, span(t), :] = jnp.where(lane_ok, value, 0.0)

        def one_step(base, tiles, chosen):
            end = tiles - 1
            for e in chosen:
                def go_south(t, here, beyond):
                    return face(south[e, t], here, beyond, fixed[base + t, 2], fixed[base + t, 3])

                start = surface[e, 0]
                final_south = go_south(end, surface[e, end], below(True, start))
                above = down(final_south)
                if not has_north:
                    above = jnp.where(first_row, (fixed[base, 0] - start) * start, above)
                here = start
                for t in range(tiles):
                    if t == end:
                        new_south = final_south
                        after = None
                    else:
                        after = surface[e, t + 1]
                        new_south = go_south(t, here, after)
                    new_east = face(
                        east[e, t], here, left(here), fixed[base + t, 1], fixed[base + t, 3]
                    )
                    change = (right(new_east) - new_east) + (above - new_south)
                    surface[e, t] = guard(jnp.maximum(here + change, fixed[base + t, 0]))
                    east[e, t] = guard(new_east)
                    south[e, t] = new_south
                    above = new_south
                    here = after

        base = 0
        for number, (first, tiles, steps) in enumerate(plan):
            if number > 0:
                old_first, old_tiles, _ = plan[number - 1]
                for e in range(events):
                    for which, ref in enumerate((surface, east, south)):
                        for t in range(old_tiles):
                            gather_back(rows.at[which, e], old_first, old_tiles, t, ref[e, t])
            for e in range(events):
                for which, ref in enumerate((surface, east, south)):
                    if number > 0 or which == 0:
                        for t in range(tiles):
                            ref[e, t] = spread(rows.at[which, e], first, tiles, t)

            def one(turn, carry, base=base, tiles=tiles):
                one_step(base, tiles, range(events))
                return carry

            def one_apart(turn, carry, base=base, tiles=tiles):
                one_step(base, tiles, (lax.rem(turn, events),))
                return carry

            if tiles <= TOGETHER_TILES:
                lax.fori_loop(0, steps, one, 0)
            else:
                lax.fori_loop(0, steps * events, one_apart, 0)
            base += tiles
        first, tiles, _ = plan[-1]
        for e in range(events):
            for t in range(tiles):
                gather_back(rows.at[0, e], first, tiles, t, surface[e, t])
            for t in range(own_tiles):
                for j in range(cols):
                    at = span(halo_tiles + t)
                    final_depth[e, span(t), piece(j)] = rows[0, e, j, at, :] - bed_rows[j, at, :]

    for copy in own_copies:
        copy.wait()

    @pl.when(r == 0)
    def _():
        flood(False, True)

    @pl.when(jnp.logical_and(r > 0, r < row_total - 1))
    def _():
        flood(True, True)

    @pl.when(r == row_total - 1)
    def _():
        flood(True, False)

    if shared:
        for index, dr in tall:
            @pl.when(row_exists(dr))
            def _():
                for array in range(3):
                    pass_on(index, array, dr).wait_send()
    for index, (dr, dc) in enumerate(REGIONS):
        @pl.when(tile_exists(-dr, -dc))
        def _():
            place_copy(index, dr, dc).wait_send()
            for array in range(3):
                strip_copy(index, array, dr, dc).wait_send()
    for rr in range(row_total):
        for dc in (-1, 0, 1):
            there = (rr != r) if dc == 0 else col_exists(dc)

            @pl.when(there)
            def _():
                level_copy(rr, dc, False).wait_send()


def body(
    row_total, col_total, cores,
    sections, send_list, send_count, slot_sender_position, block_slot_index, hand, drain, manning,
):
    events = sections.shape[0]
    tile_rows, tile_cols = hand.shape
    vmem = pl.BlockSpec(memory_space=pltpu.VMEM)
    hbm = pl.BlockSpec(memory_space=pltpu.HBM)
    padded_rows = tile_rows + 2 * HALO
    padded_tiles = padded_rows // SUBLANES
    width = tile_cols + LANES
    pieces = width // LANES
    small = (sections, send_list, send_count, slot_sender_position, block_slot_index)
    list_rows = -(-row_total // SUBLANES) * SUBLANES
    fixed_tiles = max(
        sum(tiles for tiles, _ in EDGE_STEPS), sum(tiles for tiles, _ in INNER_STEPS)
    )
    by_rows = pltpu.VMEM((pieces, padded_rows, LANES), jnp.float32)
    state = pltpu.VMEM((events, padded_tiles, SUBLANES, width), jnp.float32)
    out = jax.ShapeDtypeStruct((events, tile_rows, tile_cols), jnp.float32)
    start, end = pl.pallas_call(
        functools.partial(flood_kernel, row_total, col_total, cores),
        out_shape=(out, out),
        in_specs=[hbm] * 8,
        out_specs=(vmem, vmem),
        scratch_shapes=[pltpu.VMEM(x.shape, x.dtype) for x in small]
        + [
            pltpu.VMEM((3, padded_rows, tile_cols + 2 * LANES), jnp.float32),
            pltpu.VMEM((list_rows, LANES), jnp.int32),
            pltpu.VMEM((SUBLANES, LANES), jnp.int32),
            pltpu.VMEM((SUBLANES, LANES), jnp.int32),
            pltpu.VMEM((row_total, SUBLANES, LANES), jnp.float32),
            pltpu.VMEM((row_total, 3, SUBLANES, LANES), jnp.float32),
            pltpu.VMEM((SUBLANES, LANES), jnp.int32),
            pltpu.VMEM((3, 3, SUBLANES, LANES), jnp.int32),
            by_rows,
            by_rows,
            pltpu.VMEM((3, events, pieces, padded_rows, LANES), jnp.float32),
            state,
            state,
            state,
            pltpu.VMEM((fixed_tiles, 4, SUBLANES, width), jnp.float32),
            pltpu.SemaphoreType.DMA((len(small),)),
            pltpu.SemaphoreType.DMA((3,)),
            pltpu.SemaphoreType.DMA((len(REGIONS), 3)),
            pltpu.SemaphoreType.DMA((len(REGIONS), 3)),
            pltpu.SemaphoreType.DMA((row_total, 3)),
            pltpu.SemaphoreType.DMA((row_total, 3)),
            pltpu.SemaphoreType.DMA((len(REGIONS),)),
            pltpu.SemaphoreType.DMA((len(REGIONS),)),
            pltpu.SemaphoreType.DMA((len(REGIONS), 3)),
            pltpu.SemaphoreType.DMA((len(REGIONS), 3)),
            pltpu.SemaphoreType.REGULAR,
            pltpu.SemaphoreType.REGULAR((row_total,)),
            pltpu.SemaphoreType.REGULAR,
        ],
        compiler_params=pltpu.CompilerParams(
            collective_id=0, has_side_effects=True, vmem_limit_bytes=VMEM_BYTES
        ),
        name="flood",
    )(*[pltpu.with_memory_space_constraint(x, pltpu.HBM) for x in (*small, hand, drain, manning)])
    return start * (1.0 / SCALE), end * (1.0 / SCALE)


def solution(mesh):
    return jax.shard_map(
        functools.partial(body, mesh.shape["row"], mesh.shape["col"], mesh.shape["evt"]),
        mesh=mesh,
        in_specs=(
            P("evt", ("grp", "row", "col")),
            P(("grp", "row"), "col", None, None),
            P(("grp", "row"), "col", None),
            P(("grp", "row"), "col", None),
            P(("grp", "row"), "col"),
            P(("grp", "row"), "col"),
            P(("grp", "row"), "col"),
            P(("grp", "row"), "col"),
        ),
        out_specs=(P("evt", ("grp", "row"), "col"), P("evt", ("grp", "row"), "col")),
        check_vma=False,
    )
```

```python
import functools

import jax
import jax.numpy as jnp
from jax import lax
from jax.experimental import pallas as pl
from jax.experimental.pallas import tpu as pltpu
from jax.sharding import PartitionSpec as P

STEPS = 16
GRAVITY = 9.81
TIMESTEP = 0.4
SPACING = 10.0
DEPTH_FLOOR = 0.05
DRY_SECTION = -1000.0

VMEM_BYTES = 24 * 1024 * 1024
LANES = 128
SUBLANES = 8
HALO = STEPS
SCALE = GRAVITY * TIMESTEP * TIMESTEP / (SPACING * SPACING)
DRAG_SCALE = (
    GRAVITY * TIMESTEP * SCALE ** (7.0 / 3.0) / (SCALE * TIMESTEP / SPACING)
)
REGIONS = tuple(
    (dr, dc) for dr in (-1, 0, 1) for dc in (-1, 0, 1) if (dr, dc) != (0, 0)
)
EDGE_STEPS = ((6, 7), (5, 9))
INNER_STEPS = ((8, 3), (7, 4), (6, 4), (5, 5))

TOGETHER_TILES = 6


def phases(has_north, has_south, own_tiles):
    if has_north and has_south:
        return [
            (-(tiles - own_tiles) * SUBLANES // 2, tiles, steps) for tiles, steps in INNER_STEPS
        ]
    return [
        (-(tiles - own_tiles) * SUBLANES if has_north else 0, tiles, steps)
        for tiles, steps in EDGE_STEPS
    ]


def row_spans(dr, tile_rows):
    if dr == -1:
        return pl.ds(tile_rows - HALO, HALO), pl.ds(0, HALO)
    if dr == 1:
        return pl.ds(0, HALO), pl.ds(HALO + tile_rows, HALO)
    return pl.ds(0, tile_rows), pl.ds(HALO, tile_rows)


def col_spans(dc, tile_cols):
    if dc == -1:
        return pl.ds(tile_cols - LANES, LANES), pl.ds(tile_cols + LANES, LANES)
    if dc == 1:
        return pl.ds(0, LANES), pl.ds(tile_cols, LANES)
    return pl.ds(0, tile_cols), pl.ds(0, tile_cols)


def pick_lanes(x, index):
    return jnp.take_along_axis(x, index, axis=1, mode="promise_in_bounds")


def flood_kernel(
    row_total, col_total, cores,
    sections_in, send_list_in, send_count_in, slot_position_in, block_slot_in, hand, drain, manning,
    hand_depth, final_depth,
    sections, send_list, send_count, slot_position, block_slot,
    ext, lists, flat, slots, message, landed, place, where_held,
    bed_rows, drag_rows, rows, surface, east, south, fixed,
    small_sem, own_sem, strip_send, strip_recv, level_send, level_recv, place_send, place_recv, pass_send, pass_recv, near_sem, far_sem, sibling_sem,
):
    r = lax.axis_index("row")
    k = lax.axis_index("col")
    core = lax.axis_index("evt")
    tile_rows, tile_cols = hand.shape
    events, catch_local = sections.shape
    capacity = send_list.shape[3]
    block_rows, block_cols = block_slot.shape
    blocks = block_rows * block_cols
    cols = tile_cols // LANES
    width = tile_cols + LANES
    own_tiles = tile_rows // SUBLANES
    halo_tiles = HALO // SUBLANES
    terrain = (hand, drain, manning)
    shared = cores == 2
    share = tile_cols // 2 if shared else tile_cols
    tall = tuple((index, dr) for index, (dr, dc) in enumerate(REGIONS) if dc == 0)

    def row_exists(dr):
        return jnp.logical_and(r + dr >= 0, r + dr < row_total)

    def col_exists(dc):
        return jnp.logical_and(k + dc >= 0, k + dc < col_total)

    def tile_exists(dr, dc):
        if dr == 0:
            return col_exists(dc)
        if dc == 0:
            return row_exists(dr)
        return jnp.logical_and(row_exists(dr), col_exists(dc))

    def as_int(flag):
        return flag.astype(jnp.int32)

    earlier = ((-1, -1), (-1, 0), (-1, 1), (0, -1))
    later = ((1, -1), (1, 0), (1, 1), (0, 1))
    barrier = pltpu.get_barrier_semaphore()

    def is_earlier(rr, dc):
        there = (rr <= r) if dc == -1 else (rr < r)
        return there if dc == 0 else jnp.logical_and(there, col_exists(dc))

    def is_later(rr, dc):
        there = (rr >= r) if dc == 1 else (rr > r)
        return there if dc == 0 else jnp.logical_and(there, col_exists(dc))

    def is_near(rr, dc):
        return jnp.logical_and(rr - r <= 1, r - rr <= 1)

    partners = [(rr, dc) for rr in range(row_total) for dc in (-1, 0, 1)]

    def tell(semaphore, rr, dc):
        pl.semaphore_signal(
            semaphore, inc=1, device_id={"row": rr, "col": k + dc},
            device_id_type=pl.DeviceIdType.MESH,
        )

    for rr, dc in partners:
        @pl.when(is_later(rr, dc))
        def _():
            tell(barrier, rr, dc)

    def tell_sibling(semaphore):
        pl.semaphore_signal(
            semaphore, inc=1, device_id={"evt": 1 - core}, device_id_type=pl.DeviceIdType.MESH
        )

    if shared:
        @pl.when(core == 0)
        def _():
            tell_sibling(barrier)

    small_copies = [
        pltpu.make_async_copy(source, target, small_sem.at[at])
        for at, (source, target) in enumerate((
            (sections_in, sections), (send_list_in, send_list), (send_count_in, send_count),
            (slot_position_in, slot_position), (block_slot_in, block_slot),
        ))
    ]
    own_copies = [
        pltpu.make_async_copy(
            terrain[array], ext.at[array, pl.ds(HALO, tile_rows), pl.ds(0, tile_cols)],
            own_sem.at[array],
        )
        for array in range(3)
    ]
    for copy in small_copies + own_copies:
        copy.start()

    ahead = sum(as_int(is_earlier(rr, dc)) for rr, dc in partners)
    if shared:
        ahead = ahead + as_int(core == 1)

    @pl.when(ahead > 0)
    def _():
        pl.semaphore_wait(barrier, ahead)

    if shared:
        @pl.when(core == 1)
        def _():
            tell_sibling(sibling_sem)

    for rr, dc in partners:
        @pl.when(jnp.logical_and(is_earlier(rr, dc), is_near(rr, dc)))
        def _():
            tell(near_sem, rr, dc)

        @pl.when(jnp.logical_and(is_earlier(rr, dc), jnp.logical_not(is_near(rr, dc))))
        def _():
            tell(far_sem.at[r], rr, dc)

    def strip_copy(index, array, dr, dc):
        src_rows, dst_rows = row_spans(dr, tile_rows)
        src_cols, dst_cols = col_spans(dc, tile_cols)
        if dc == 0:
            src_cols = dst_cols = pl.ds(pl.multiple_of(core * share, LANES) if shared else 0, share)
        return pltpu.make_async_remote_copy(
            src_ref=terrain[array].at[src_rows, src_cols],
            dst_ref=ext.at[array, dst_rows, dst_cols],
            send_sem=strip_send.at[index, array],
            recv_sem=strip_recv.at[index, array],
            device_id={"row": r - dr, "col": k - dc},
            device_id_type=pl.DeviceIdType.MESH,
        )

    def pass_on(index, array, dr):
        held = ext.at[
            array, row_spans(dr, tile_rows)[1], pl.ds(pl.multiple_of(core * share, LANES), share)
        ]
        return pltpu.make_async_remote_copy(
            src_ref=held,
            dst_ref=held,
            send_sem=pass_send.at[index, array],
            recv_sem=pass_recv.at[index, array],
            device_id={"evt": 1 - core},
            device_id_type=pl.DeviceIdType.MESH,
        )

    def send_strips(targets):
        for index, (dr, dc) in sorted(enumerate(REGIONS), key=lambda entry: entry[1][1] != 0):
            if (-dr, -dc) in targets:
                @pl.when(tile_exists(-dr, -dc))
                def _():
                    for array in range(3):
                        strip_copy(index, array, dr, dc).start()

    @pl.when(r < row_total - 1)
    def _():
        send_strips(earlier)

    lane = lax.broadcasted_iota(jnp.int32, (SUBLANES, LANES), 1)
    row_id = lax.broadcasted_iota(jnp.int32, (SUBLANES, LANES), 0)
    near = lane < LANES // 2
    lists[...] = jnp.zeros(lists.shape, jnp.int32)
    flat[...] = jnp.zeros(flat.shape, jnp.int32)
    slots[...] = jnp.zeros(slots.shape, jnp.int32)
    for copy in small_copies:
        copy.wait()

    lane_of = lax.broadcasted_iota(jnp.int32, (1, capacity), 1)
    for rr in range(row_total):
        live = lane_of < jnp.broadcast_to(send_count[0, :, rr : rr + 1], (1, capacity))
        held = jnp.where(live, send_list[0, 0, rr : rr + 1, :], -1)
        for e in range(events):
            lists[rr : rr + 1, e * capacity : (e + 1) * capacity] = held
    list_rows = lists.shape[0]
    lane_tall = lax.broadcasted_iota(jnp.int32, (list_rows, LANES), 1)
    wanted = lists[...]
    local = jnp.maximum(wanted, 0)
    values = jnp.full((list_rows, LANES), DRY_SECTION, jnp.float32)
    for half in range(catch_local // LANES):
        mine = jnp.logical_and(wanted >= half * LANES, wanted < (half + 1) * LANES)
        for e in range(events):
            source = jnp.broadcast_to(
                sections[e : e + 1, half * LANES : (half + 1) * LANES], (list_rows, LANES)
            )
            found = pick_lanes(source, jnp.bitwise_and(local, LANES - 1))
            of_event = jnp.logical_and(lane_tall >= e * capacity, lane_tall < (e + 1) * capacity)
            values = jnp.where(jnp.logical_and(mine, of_event), found, values)
    for rr in range(row_total):
        message[rr] = jnp.full((SUBLANES, LANES), DRY_SECTION, jnp.float32)
        for j in (-1, 0, 1):
            pick = min(max(rr + j, 0), row_total - 1)
            message[rr, j + 1 : j + 2, :] = values[pick : pick + 1, :]

    def level_copy(rr, dc, arriving):
        at = (rr, 1 + dc) if arriving else (r, 1 - dc)
        return pltpu.make_async_remote_copy(
            src_ref=message.at[rr],
            dst_ref=landed.at[at],
            send_sem=level_send.at[rr, dc + 1],
            recv_sem=level_recv.at[at],
            device_id={"row": rr, "col": k + dc},
            device_id_type=pl.DeviceIdType.MESH,
        )

    def place_copy(index, dr, dc):
        return pltpu.make_async_remote_copy(
            src_ref=place,
            dst_ref=where_held.at[1 + dr, 1 + dc],
            send_sem=place_send.at[index],
            recv_sem=place_recv.at[index],
            device_id={"row": r - dr, "col": k - dc},
            device_id_type=pl.DeviceIdType.MESH,
        )

    def send_levels(chosen):
        for rr, dc in partners:
            @pl.when(chosen(rr, dc))
            def _():
                level_copy(rr, dc, False).start()

    def send_place(targets):
        for index, (dr, dc) in enumerate(REGIONS):
            if (-dr, -dc) in targets:
                @pl.when(tile_exists(-dr, -dc))
                def _():
                    place_copy(index, dr, dc).start()

    send_levels(is_earlier)

    slots[0:1, 0 : slot_position.shape[2]] = slot_position[0]
    for e in range(events):
        for row in range(block_rows):
            at = e * blocks + row * block_cols
            flat[0:1, at : at + block_cols] = block_slot[row : row + 1, :]
    tile_shape = (SUBLANES, LANES)
    own_place = pick_lanes(
        jnp.broadcast_to(slots[0:1, :], tile_shape), jnp.broadcast_to(flat[0:1, :], tile_shape)
    )
    place[...] = own_place
    where_held[1, 1] = own_place

    send_place(earlier)

    @pl.when(r == row_total - 1)
    def _():
        send_strips(earlier)

    behind = sum(as_int(tile_exists(dr, dc)) for dr, dc in later)

    @pl.when(behind > 0)
    def _():
        pl.semaphore_wait(near_sem, behind)

    send_levels(lambda rr, dc: jnp.logical_and(is_later(rr, dc), is_near(rr, dc)))
    send_strips(later)
    send_place(later)
    reach = sum(as_int(col_exists(dc)) for dc in (-1, 0, 1))
    for row in range(row_total):
        @pl.when(row > r + 1)
        def _():
            pl.semaphore_wait(far_sem.at[row], reach)

            for rr, dc in partners:
                if rr == row:
                    @pl.when(is_later(rr, dc))
                    def _():
                        level_copy(rr, dc, False).start()

    landed[r, 1] = message[r]

    lane_ok = jnp.where(near, as_int(col_exists(1)), as_int(col_exists(-1))) > 0
    wide_row = lax.broadcasted_iota(jnp.int32, (SUBLANES, width), 0)
    last_row = wide_row == SUBLANES - 1
    first_row = wide_row == 0

    def span(t):
        return pl.ds(t * SUBLANES, SUBLANES)

    def piece(j):
        return slice(j * LANES, (j + 1) * LANES)

    def up(x):
        return pltpu.roll(x, SUBLANES - 1, 0)

    def down(x):
        return pltpu.roll(x, 1, 0)

    def left(x):
        return pltpu.roll(x, width - 1, 1)

    def right(x):
        return pltpu.roll(x, 1, 1)

    def guard(x):
        return jnp.concatenate(
            [x[:, :tile_cols], jnp.where(lane_ok, x[:, tile_cols:], 0.0)], 1
        )

    def beside(array, t):
        return jnp.where(
            near,
            ext[array, span(t), tile_cols : tile_cols + LANES],
            ext[array, span(t), tile_cols + LANES : tile_cols + 2 * LANES],
        )

    def set_terrain(t, side):
        if side:
            height, low, rough = [beside(array, t) for array in range(3)]
            bed_rows[cols, span(t), :] = jnp.where(lane_ok, SCALE * (height + low), 0.0)
            drag_rows[cols, span(t), :] = jnp.where(lane_ok, DRAG_SCALE * (rough * rough), 0.0)
            return
        for j in range(cols):
            height, low, rough = [ext[array, span(t), piece(j)] for array in range(3)]
            bed_rows[j, span(t), :] = SCALE * (height + low)
            drag_rows[j, span(t), :] = DRAG_SCALE * (rough * rough)

    def spread(ref, first, tiles, t):
        return jnp.concatenate(
            [ref[j, pl.ds(first + t, SUBLANES, stride=tiles), :] for j in range(cols + 1)], 1
        )

    def gather_back(ref, first, tiles, t, x):
        for j in range(cols + 1):
            ref[j, pl.ds(first + t, SUBLANES, stride=tiles), :] = x[:, piece(j)]

    def level_of(held, dr, lane_at):
        return jnp.broadcast_to(held[dr + 1 : dr + 2, lane_at : lane_at + 1], tile_shape)

    def face(flow, here, beyond, top, rough):
        thick = jnp.maximum(here, beyond) - top
        power = jnp.exp2((-7.0 / 3.0) * jnp.log2(jnp.maximum(thick, SCALE * DEPTH_FLOOR)))
        pushed = flow - thick * (beyond - here)
        return pushed * pl.reciprocal(1.0 + rough * jnp.abs(flow) * power, approx=True)

    def flood(has_north, has_south):
        plan = [(first + HALO, tiles, steps) for first, tiles, steps in phases(has_north, has_south, own_tiles)]
        row_tiles = range(
            0 if has_north else halo_tiles,
            halo_tiles + own_tiles + (halo_tiles if has_south else 0),
        )

        def below(bottom, x):
            x = up(x)
            return x if has_south else jnp.where(last_row, 0.0, x)

        for t in range(halo_tiles, halo_tiles + own_tiles):
            set_terrain(t, False)
        for t in range(plan[0][1]):
            for e in range(events):
                east[e, t] = jnp.zeros((SUBLANES, width), jnp.float32)
                south[e, t] = jnp.zeros((SUBLANES, width), jnp.float32)

        halos = [(index, dr) for index, dr in tall if (has_north if dr == -1 else has_south)]
        if shared:
            @pl.when(core == 0)
            def _():
                pl.semaphore_wait(sibling_sem, 1)

        for array in range(3):
            for index, dr in halos:
                strip_copy(index, array, dr, 0).wait_recv()
                if shared:
                    pass_on(index, array, dr).start()
        for index, (dr, dc) in enumerate(REGIONS):
            if (dr == -1 and not has_north) or (dr == 1 and not has_south):
                continue

            @pl.when(col_exists(dc))
            def _():
                place_copy(index, dr, dc).wait_recv()
        for rr in range(row_total):
            for dc in (-1, 0, 1):
                there = (rr != r) if dc == 0 else col_exists(dc)

                @pl.when(there)
                def _():
                    level_copy(rr, dc, True).wait_recv()

        event_shift = jnp.where(lane >= blocks, capacity, 0)
        levels = []
        for kc in range(3):
            placed = jnp.where(
                row_id == 0, where_held[0, kc], jnp.where(row_id == 1, where_held[1, kc], where_held[2, kc])
            )
            source = lax.shift_right_logical(placed, capacity.bit_length() - 1)
            at = jnp.bitwise_and(placed, capacity - 1) + event_shift
            level = jnp.full(tile_shape, DRY_SECTION, jnp.float32)
            for rr in range(row_total):
                level = jnp.where(source == rr, pick_lanes(landed[rr, kc], at), level)
            levels.append(level)

        def block_at(e, t):
            dr, row = 0, t - halo_tiles
            if t < halo_tiles:
                dr, row = -1, block_rows - halo_tiles + t
            elif row >= own_tiles:
                dr, row = 1, row - own_tiles
            return dr, row, e * blocks + row * block_cols

        def set_surface(t):
            for e in range(events):
                dr, row, at = block_at(e, t)
                for j in range(cols):
                    value = SCALE * jnp.maximum(
                        level_of(levels[1], dr, at + j) - ext[0, span(t), piece(j)], 0.0
                    )
                    if dr == 0:
                        hand_depth[e, span(row), piece(j)] = value
                    rows[0, e, j, span(t), :] = value + bed_rows[j, span(t), :]

        def set_side_surface(t):
            side_height = beside(0, t)
            for e in range(events):
                dr, row, at = block_at(e, t)
                level = jnp.where(
                    near, level_of(levels[2], dr, at), level_of(levels[0], dr, at + block_cols - 1)
                )
                value = SCALE * jnp.maximum(level - side_height, 0.0) + bed_rows[cols, span(t), :]
                rows[0, e, cols, span(t), :] = jnp.where(lane_ok, value, 0.0)

        own_range = range(halo_tiles, halo_tiles + own_tiles)
        for t in own_range:
            set_surface(t)
        for index, (dr, dc) in enumerate(REGIONS):
            if dc == 0 or (dr == -1 and not has_north) or (dr == 1 and not has_south):
                continue

            @pl.when(col_exists(dc))
            def _():
                for array in range(3):
                    strip_copy(index, array, dr, dc).wait_recv()
        for t in row_tiles:
            set_terrain(t, True)
            set_side_surface(t)
        if shared:
            for array in range(3):
                for index, dr in halos:
                    pass_on(index, array, dr).wait_recv()
        for t in row_tiles:
            if t not in own_range:
                set_terrain(t, False)
                set_surface(t)

        base = 0
        for first, tiles, _ in plan:
            start = spread(bed_rows, first, tiles, 0)
            here = start
            for t in range(tiles):
                after = below(True, start) if t == tiles - 1 else spread(bed_rows, first, tiles, t + 1)
                fixed[base + t, 0] = here
                fixed[base + t, 1] = jnp.maximum(here, left(here))
                fixed[base + t, 2] = jnp.maximum(here, after)
                fixed[base + t, 3] = spread(drag_rows, first, tiles, t)
                here = after
            base += tiles
        def one_step(base, tiles, chosen):
            end = tiles - 1
            for e in chosen:
                def go_south(t, here, beyond):
                    return face(south[e, t], here, beyond, fixed[base + t, 2], fixed[base + t, 3])

                start = surface[e, 0]
                final_south = go_south(end, surface[e, end], below(True, start))
                above = down(final_south)
                if not has_north:
                    above = jnp.where(first_row, (fixed[base, 0] - start) * start, above)
                here = start
                for t in range(tiles):
                    if t == end:
                        new_south = final_south
                        after = None
                    else:
                        after = surface[e, t + 1]
                        new_south = go_south(t, here, after)
                    new_east = face(
                        east[e, t], here, left(here), fixed[base + t, 1], fixed[base + t, 3]
                    )
                    change = (right(new_east) - new_east) + (above - new_south)
                    surface[e, t] = guard(jnp.maximum(here + change, fixed[base + t, 0]))
                    east[e, t] = guard(new_east)
                    south[e, t] = new_south
                    above = new_south
                    here = after

        base = 0
        for number, (first, tiles, steps) in enumerate(plan):
            if number > 0:
                old_first, old_tiles, _ = plan[number - 1]
                for e in range(events):
                    for which, ref in enumerate((surface, east, south)):
                        for t in range(old_tiles):
                            gather_back(rows.at[which, e], old_first, old_tiles, t, ref[e, t])
            for e in range(events):
                for which, ref in enumerate((surface, east, south)):
                    if number > 0 or which == 0:
                        for t in range(tiles):
                            ref[e, t] = spread(rows.at[which, e], first, tiles, t)

            def one(turn, carry, base=base, tiles=tiles):
                one_step(base, tiles, range(events))
                return carry

            def one_apart(turn, carry, base=base, tiles=tiles):
                one_step(base, tiles, (lax.rem(turn, events),))
                return carry

            if tiles <= TOGETHER_TILES:
                lax.fori_loop(0, steps, one, 0)
            else:
                lax.fori_loop(0, steps * events, one_apart, 0)
            base += tiles
        first, tiles, _ = plan[-1]
        for e in range(events):
            for t in range(tiles):
                gather_back(rows.at[0, e], first, tiles, t, surface[e, t])
            for t in range(own_tiles):
                for j in range(cols):
                    at = span(halo_tiles + t)
                    final_depth[e, span(t), piece(j)] = rows[0, e, j, at, :] - bed_rows[j, at, :]

    for copy in own_copies:
        copy.wait()

    @pl.when(r == 0)
    def _():
        flood(False, True)

    @pl.when(jnp.logical_and(r > 0, r < row_total - 1))
    def _():
        flood(True, True)

    @pl.when(r == row_total - 1)
    def _():
        flood(True, False)

    if shared:
        for index, dr in tall:
            @pl.when(row_exists(dr))
            def _():
                for array in range(3):
                    pass_on(index, array, dr).wait_send()
    for index, (dr, dc) in enumerate(REGIONS):
        @pl.when(tile_exists(-dr, -dc))
        def _():
            place_copy(index, dr, dc).wait_send()
            for array in range(3):
                strip_copy(index, array, dr, dc).wait_send()
    for rr in range(row_total):
        for dc in (-1, 0, 1):
            there = (rr != r) if dc == 0 else col_exists(dc)

            @pl.when(there)
            def _():
                level_copy(rr, dc, False).wait_send()


def body(
    row_total, col_total, cores,
    sections, send_list, send_count, slot_sender_position, block_slot_index, hand, drain, manning,
):
    events = sections.shape[0]
    tile_rows, tile_cols = hand.shape
    vmem = pl.BlockSpec(memory_space=pltpu.VMEM)
    hbm = pl.BlockSpec(memory_space=pltpu.HBM)
    padded_rows = tile_rows + 2 * HALO
    padded_tiles = padded_rows // SUBLANES
    width = tile_cols + LANES
    pieces = width // LANES
    small = (sections, send_list, send_count, slot_sender_position, block_slot_index)
    list_rows = -(-row_total // SUBLANES) * SUBLANES
    fixed_tiles = max(
        sum(tiles for tiles, _ in EDGE_STEPS), sum(tiles for tiles, _ in INNER_STEPS)
    )
    by_rows = pltpu.VMEM((pieces, padded_rows, LANES), jnp.float32)
    state = pltpu.VMEM((events, padded_tiles, SUBLANES, width), jnp.float32)
    out = jax.ShapeDtypeStruct((events, tile_rows, tile_cols), jnp.float32)
    start, end = pl.pallas_call(
        functools.partial(flood_kernel, row_total, col_total, cores),
        out_shape=(out, out),
        in_specs=[hbm] * 8,
        out_specs=(vmem, vmem),
        scratch_shapes=[pltpu.VMEM(x.shape, x.dtype) for x in small]
        + [
            pltpu.VMEM((3, padded_rows, tile_cols + 2 * LANES), jnp.float32),
            pltpu.VMEM((list_rows, LANES), jnp.int32),
            pltpu.VMEM((SUBLANES, LANES), jnp.int32),
            pltpu.VMEM((SUBLANES, LANES), jnp.int32),
            pltpu.VMEM((row_total, SUBLANES, LANES), jnp.float32),
            pltpu.VMEM((row_total, 3, SUBLANES, LANES), jnp.float32),
            pltpu.VMEM((SUBLANES, LANES), jnp.int32),
            pltpu.VMEM((3, 3, SUBLANES, LANES), jnp.int32),
            by_rows,
            by_rows,
            pltpu.VMEM((3, events, pieces, padded_rows, LANES), jnp.float32),
            state,
            state,
            state,
            pltpu.VMEM((fixed_tiles, 4, SUBLANES, width), jnp.float32),
            pltpu.SemaphoreType.DMA((len(small),)),
            pltpu.SemaphoreType.DMA((3,)),
            pltpu.SemaphoreType.DMA((len(REGIONS), 3)),
            pltpu.SemaphoreType.DMA((len(REGIONS), 3)),
            pltpu.SemaphoreType.DMA((row_total, 3)),
            pltpu.SemaphoreType.DMA((row_total, 3)),
            pltpu.SemaphoreType.DMA((len(REGIONS),)),
            pltpu.SemaphoreType.DMA((len(REGIONS),)),
            pltpu.SemaphoreType.DMA((len(REGIONS), 3)),
            pltpu.SemaphoreType.DMA((len(REGIONS), 3)),
            pltpu.SemaphoreType.REGULAR,
            pltpu.SemaphoreType.REGULAR((row_total,)),
            pltpu.SemaphoreType.REGULAR,
        ],
        compiler_params=pltpu.CompilerParams(
            collective_id=0, has_side_effects=True, vmem_limit_bytes=VMEM_BYTES
        ),
        name="flood",
    )(*[pltpu.with_memory_space_constraint(x, pltpu.HBM) for x in (*small, hand, drain, manning)])
    return start * (1.0 / SCALE), end * (1.0 / SCALE)


def solution(mesh):
    return jax.shard_map(
        functools.partial(body, mesh.shape["row"], mesh.shape["col"], mesh.shape["evt"]),
        mesh=mesh,
        in_specs=(
            P("evt", ("grp", "row", "col")),
            P(("grp", "row"), "col", None, None),
            P(("grp", "row"), "col", None),
            P(("grp", "row"), "col", None),
            P(("grp", "row"), "col"),
            P(("grp", "row"), "col"),
            P(("grp", "row"), "col"),
            P(("grp", "row"), "col"),
        ),
        out_specs=(P("evt", ("grp", "row"), "col"), P("evt", ("grp", "row"), "col")),
        check_vma=False,
    )
```

```python
import functools

import jax
import jax.numpy as jnp
from jax import lax
from jax.experimental import pallas as pl
from jax.experimental.pallas import tpu as pltpu
from jax.sharding import PartitionSpec as P

STEPS = 16
GRAVITY = 9.81
TIMESTEP = 0.4
SPACING = 10.0
DEPTH_FLOOR = 0.05
DRY_SECTION = -1000.0

VMEM_BYTES = 24 * 1024 * 1024
LANES = 128
SUBLANES = 8
HALO = STEPS
SCALE = GRAVITY * TIMESTEP * TIMESTEP / (SPACING * SPACING)
DRAG_SCALE = (
    GRAVITY * TIMESTEP * SCALE ** (7.0 / 3.0) / (SCALE * TIMESTEP / SPACING)
)
REGIONS = tuple(
    (dr, dc) for dr in (-1, 0, 1) for dc in (-1, 0, 1) if (dr, dc) != (0, 0)
)
EDGE_STEPS = ((6, 7), (5, 9))
INNER_STEPS = ((8, 3), (7, 4), (6, 4), (5, 5))

TOGETHER_TILES = 5


def phases(has_north, has_south, own_tiles):
    if has_north and has_south:
        return [
            (-(tiles - own_tiles) * SUBLANES // 2, tiles, steps) for tiles, steps in INNER_STEPS
        ]
    return [
        (-(tiles - own_tiles) * SUBLANES if has_north else 0, tiles, steps)
        for tiles, steps in EDGE_STEPS
    ]


def row_spans(dr, tile_rows):
    if dr == -1:
        return pl.ds(tile_rows - HALO, HALO), pl.ds(0, HALO)
    if dr == 1:
        return pl.ds(0, HALO), pl.ds(HALO + tile_rows, HALO)
    return pl.ds(0, tile_rows), pl.ds(HALO, tile_rows)


def col_spans(dc, tile_cols):
    if dc == -1:
        return pl.ds(tile_cols - LANES, LANES), pl.ds(tile_cols + LANES, LANES)
    if dc == 1:
        return pl.ds(0, LANES), pl.ds(tile_cols, LANES)
    return pl.ds(0, tile_cols), pl.ds(0, tile_cols)


def pick_lanes(x, index):
    return jnp.take_along_axis(x, index, axis=1, mode="promise_in_bounds")


def flood_kernel(
    row_total, col_total, cores,
    sections_in, send_list_in, send_count_in, slot_position_in, block_slot_in, hand, drain, manning,
    hand_depth, final_depth,
    sections, send_list, send_count, slot_position, block_slot,
    ext, lists, flat, slots, message, landed, place, where_held,
    bed_rows, drag_rows, rows, surface, east, south, fixed,
    small_sem, own_sem, strip_send, strip_recv, level_send, level_recv, place_send, place_recv, pass_send, pass_recv, near_sem, far_sem, sibling_sem,
):
    r = lax.axis_index("row")
    k = lax.axis_index("col")
    core = lax.axis_index("evt")
    tile_rows, tile_cols = hand.shape
    events, catch_local = sections.shape
    capacity = send_list.shape[3]
    block_rows, block_cols = block_slot.shape
    blocks = block_rows * block_cols
    cols = tile_cols // LANES
    width = tile_cols + LANES
    own_tiles = tile_rows // SUBLANES
    halo_tiles = HALO // SUBLANES
    terrain = (hand, drain, manning)
    shared = cores == 2
    share = tile_cols // 2 if shared else tile_cols
    tall = tuple((index, dr) for index, (dr, dc) in enumerate(REGIONS) if dc == 0)

    def row_exists(dr):
        return jnp.logical_and(r + dr >= 0, r + dr < row_total)

    def col_exists(dc):
        return jnp.logical_and(k + dc >= 0, k + dc < col_total)

    def tile_exists(dr, dc):
        if dr == 0:
            return col_exists(dc)
        if dc == 0:
            return row_exists(dr)
        return jnp.logical_and(row_exists(dr), col_exists(dc))

    def as_int(flag):
        return flag.astype(jnp.int32)

    earlier = ((-1, -1), (-1, 0), (-1, 1), (0, -1))
    later = ((1, -1), (1, 0), (1, 1), (0, 1))
    barrier = pltpu.get_barrier_semaphore()

    def is_earlier(rr, dc):
        there = (rr <= r) if dc == -1 else (rr < r)
        return there if dc == 0 else jnp.logical_and(there, col_exists(dc))

    def is_later(rr, dc):
        there = (rr >= r) if dc == 1 else (rr > r)
        return there if dc == 0 else jnp.logical_and(there, col_exists(dc))

    def is_near(rr, dc):
        return jnp.logical_and(rr - r <= 1, r - rr <= 1)

    partners = [(rr, dc) for rr in range(row_total) for dc in (-1, 0, 1)]

    def tell(semaphore, rr, dc):
        pl.semaphore_signal(
            semaphore, inc=1, device_id={"row": rr, "col": k + dc},
            device_id_type=pl.DeviceIdType.MESH,
        )

    for rr, dc in partners:
        @pl.when(is_later(rr, dc))
        def _():
            tell(barrier, rr, dc)

    def tell_sibling(semaphore):
        pl.semaphore_signal(
            semaphore, inc=1, device_id={"evt": 1 - core}, device_id_type=pl.DeviceIdType.MESH
        )

    if shared:
        @pl.when(core == 0)
        def _():
            tell_sibling(barrier)

    small_copies = [
        pltpu.make_async_copy(source, target, small_sem.at[at])
        for at, (source, target) in enumerate((
            (sections_in, sections), (send_list_in, send_list), (send_count_in, send_count),
            (slot_position_in, slot_position), (block_slot_in, block_slot),
        ))
    ]
    own_copies = [
        pltpu.make_async_copy(
            terrain[array], ext.at[array, pl.ds(HALO, tile_rows), pl.ds(0, tile_cols)],
            own_sem.at[array],
        )
        for array in range(3)
    ]
    for copy in small_copies + own_copies:
        copy.start()

    ahead = sum(as_int(is_earlier(rr, dc)) for rr, dc in partners)
    if shared:
        ahead = ahead + as_int(core == 1)

    @pl.when(ahead > 0)
    def _():
        pl.semaphore_wait(barrier, ahead)

    if shared:
        @pl.when(core == 1)
        def _():
            tell_sibling(sibling_sem)

    for rr, dc in partners:
        @pl.when(jnp.logical_and(is_earlier(rr, dc), is_near(rr, dc)))
        def _():
            tell(near_sem, rr, dc)

        @pl.when(jnp.logical_and(is_earlier(rr, dc), jnp.logical_not(is_near(rr, dc))))
        def _():
            tell(far_sem.at[r], rr, dc)

    def strip_copy(index, array, dr, dc):
        src_rows, dst_rows = row_spans(dr, tile_rows)
        src_cols, dst_cols = col_spans(dc, tile_cols)
        if dc == 0:
            src_cols = dst_cols = pl.ds(pl.multiple_of(core * share, LANES) if shared else 0, share)
        return pltpu.make_async_remote_copy(
            src_ref=terrain[array].at[src_rows, src_cols],
            dst_ref=ext.at[array, dst_rows, dst_cols],
            send_sem=strip_send.at[index, array],
            recv_sem=strip_recv.at[index, array],
            device_id={"row": r - dr, "col": k - dc},
            device_id_type=pl.DeviceIdType.MESH,
        )

    def pass_on(index, array, dr):
        held = ext.at[
            array, row_spans(dr, tile_rows)[1], pl.ds(pl.multiple_of(core * share, LANES), share)
        ]
        return pltpu.make_async_remote_copy(
            src_ref=held,
            dst_ref=held,
            send_sem=pass_send.at[index, array],
            recv_sem=pass_recv.at[index, array],
            device_id={"evt": 1 - core},
            device_id_type=pl.DeviceIdType.MESH,
        )

    def send_strips(targets):
        for index, (dr, dc) in sorted(enumerate(REGIONS), key=lambda entry: entry[1][1] != 0):
            if (-dr, -dc) in targets:
                @pl.when(tile_exists(-dr, -dc))
                def _():
                    for array in range(3):
                        strip_copy(index, array, dr, dc).start()


    lane = lax.broadcasted_iota(jnp.int32, (SUBLANES, LANES), 1)
    row_id = lax.broadcasted_iota(jnp.int32, (SUBLANES, LANES), 0)
    near = lane < LANES // 2
    lists[...] = jnp.zeros(lists.shape, jnp.int32)
    flat[...] = jnp.zeros(flat.shape, jnp.int32)
    slots[...] = jnp.zeros(slots.shape, jnp.int32)
    for copy in small_copies:
        copy.wait()

    lane_of = lax.broadcasted_iota(jnp.int32, (1, capacity), 1)
    for rr in range(row_total):
        live = lane_of < jnp.broadcast_to(send_count[0, :, rr : rr + 1], (1, capacity))
        held = jnp.where(live, send_list[0, 0, rr : rr + 1, :], -1)
        for e in range(events):
            lists[rr : rr + 1, e * capacity : (e + 1) * capacity] = held
    list_rows = lists.shape[0]
    lane_tall = lax.broadcasted_iota(jnp.int32, (list_rows, LANES), 1)
    wanted = lists[...]
    local = jnp.maximum(wanted, 0)
    values = jnp.full((list_rows, LANES), DRY_SECTION, jnp.float32)
    for half in range(catch_local // LANES):
        mine = jnp.logical_and(wanted >= half * LANES, wanted < (half + 1) * LANES)
        for e in range(events):
            source = jnp.broadcast_to(
                sections[e : e + 1, half * LANES : (half + 1) * LANES], (list_rows, LANES)
            )
            found = pick_lanes(source, jnp.bitwise_and(local, LANES - 1))
            of_event = jnp.logical_and(lane_tall >= e * capacity, lane_tall < (e + 1) * capacity)
            values = jnp.where(jnp.logical_and(mine, of_event), found, values)
    for rr in range(row_total):
        message[rr] = jnp.full((SUBLANES, LANES), DRY_SECTION, jnp.float32)
        for j in (-1, 0, 1):
            pick = min(max(rr + j, 0), row_total - 1)
            message[rr, j + 1 : j + 2, :] = values[pick : pick + 1, :]

    def level_copy(rr, dc, arriving):
        at = (rr, 1 + dc) if arriving else (r, 1 - dc)
        return pltpu.make_async_remote_copy(
            src_ref=message.at[rr],
            dst_ref=landed.at[at],
            send_sem=level_send.at[rr, dc + 1],
            recv_sem=level_recv.at[at],
            device_id={"row": rr, "col": k + dc},
            device_id_type=pl.DeviceIdType.MESH,
        )

    def place_copy(index, dr, dc):
        return pltpu.make_async_remote_copy(
            src_ref=place,
            dst_ref=where_held.at[1 + dr, 1 + dc],
            send_sem=place_send.at[index],
            recv_sem=place_recv.at[index],
            device_id={"row": r - dr, "col": k - dc},
            device_id_type=pl.DeviceIdType.MESH,
        )

    def send_levels(chosen):
        for rr, dc in partners:
            @pl.when(chosen(rr, dc))
            def _():
                level_copy(rr, dc, False).start()

    def send_place(targets):
        for index, (dr, dc) in enumerate(REGIONS):
            if (-dr, -dc) in targets:
                @pl.when(tile_exists(-dr, -dc))
                def _():
                    place_copy(index, dr, dc).start()

    send_levels(is_earlier)

    slots[0:1, 0 : slot_position.shape[2]] = slot_position[0]
    for e in range(events):
        for row in range(block_rows):
            at = e * blocks + row * block_cols
            flat[0:1, at : at + block_cols] = block_slot[row : row + 1, :]
    tile_shape = (SUBLANES, LANES)
    own_place = pick_lanes(
        jnp.broadcast_to(slots[0:1, :], tile_shape), jnp.broadcast_to(flat[0:1, :], tile_shape)
    )
    place[...] = own_place
    where_held[1, 1] = own_place

    send_place(earlier)

    send_strips(earlier)

    behind = sum(as_int(tile_exists(dr, dc)) for dr, dc in later)

    @pl.when(behind > 0)
    def _():
        pl.semaphore_wait(near_sem, behind)

    send_levels(lambda rr, dc: jnp.logical_and(is_later(rr, dc), is_near(rr, dc)))
    send_place(later)
    send_strips(later)
    reach = sum(as_int(col_exists(dc)) for dc in (-1, 0, 1))
    for row in range(row_total):
        @pl.when(row > r + 1)
        def _():
            pl.semaphore_wait(far_sem.at[row], reach)

            for rr, dc in partners:
                if rr == row:
                    @pl.when(is_later(rr, dc))
                    def _():
                        level_copy(rr, dc, False).start()

    landed[r, 1] = message[r]

    lane_ok = jnp.where(near, as_int(col_exists(1)), as_int(col_exists(-1))) > 0
    wide_row = lax.broadcasted_iota(jnp.int32, (SUBLANES, width), 0)
    last_row = wide_row == SUBLANES - 1
    first_row = wide_row == 0

    def span(t):
        return pl.ds(t * SUBLANES, SUBLANES)

    def piece(j):
        return slice(j * LANES, (j + 1) * LANES)

    def up(x):
        return pltpu.roll(x, SUBLANES - 1, 0)

    def down(x):
        return pltpu.roll(x, 1, 0)

    def left(x):
        return pltpu.roll(x, width - 1, 1)

    def right(x):
        return pltpu.roll(x, 1, 1)

    def guard(x):
        return jnp.concatenate(
            [x[:, :tile_cols], jnp.where(lane_ok, x[:, tile_cols:], 0.0)], 1
        )

    def beside(array, t):
        return jnp.where(
            near,
            ext[array, span(t), tile_cols : tile_cols + LANES],
            ext[array, span(t), tile_cols + LANES : tile_cols + 2 * LANES],
        )

    def set_terrain(t, side):
        if side:
            height, low, rough = [beside(array, t) for array in range(3)]
            bed_rows[cols, span(t), :] = jnp.where(lane_ok, SCALE * (height + low), 0.0)
            drag_rows[cols, span(t), :] = jnp.where(lane_ok, DRAG_SCALE * (rough * rough), 0.0)
            return
        for j in range(cols):
            height, low, rough = [ext[array, span(t), piece(j)] for array in range(3)]
            bed_rows[j, span(t), :] = SCALE * (height + low)
            drag_rows[j, span(t), :] = DRAG_SCALE * (rough * rough)

    def spread(ref, first, tiles, t):
        return jnp.concatenate(
            [ref[j, pl.ds(first + t, SUBLANES, stride=tiles), :] for j in range(cols + 1)], 1
        )

    def gather_back(ref, first, tiles, t, x):
        for j in range(cols + 1):
            ref[j, pl.ds(first + t, SUBLANES, stride=tiles), :] = x[:, piece(j)]

    def level_of(held, dr, lane_at):
        return jnp.broadcast_to(held[dr + 1 : dr + 2, lane_at : lane_at + 1], tile_shape)

    def face(flow, here, beyond, top, rough):
        thick = jnp.maximum(here, beyond) - top
        power = jnp.exp2((-7.0 / 3.0) * jnp.log2(jnp.maximum(thick, SCALE * DEPTH_FLOOR)))
        pushed = flow - thick * (beyond - here)
        return pushed * pl.reciprocal(1.0 + rough * jnp.abs(flow) * power, approx=True)

    def flood(has_north, has_south):
        plan = [(first + HALO, tiles, steps) for first, tiles, steps in phases(has_north, has_south, own_tiles)]
        row_tiles = range(
            0 if has_north else halo_tiles,
            halo_tiles + own_tiles + (halo_tiles if has_south else 0),
        )

        def below(bottom, x):
            x = up(x)
            return x if has_south else jnp.where(last_row, 0.0, x)

        for t in range(halo_tiles, halo_tiles + own_tiles):
            set_terrain(t, False)
        for t in range(plan[0][1]):
            for e in range(events):
                east[e, t] = jnp.zeros((SUBLANES, width), jnp.float32)
                south[e, t] = jnp.zeros((SUBLANES, width), jnp.float32)

        halos = [(index, dr) for index, dr in tall if (has_north if dr == -1 else has_south)]
        if shared:
            @pl.when(core == 0)
            def _():
                pl.semaphore_wait(sibling_sem, 1)

        for array in range(3):
            for index, dr in halos:
                strip_copy(index, array, dr, 0).wait_recv()
                if shared:
                    pass_on(index, array, dr).start()
        for index, (dr, dc) in enumerate(REGIONS):
            if (dr == -1 and not has_north) or (dr == 1 and not has_south):
                continue

            @pl.when(col_exists(dc))
            def _():
                place_copy(index, dr, dc).wait_recv()
        for rr in range(row_total):
            for dc in (-1, 0, 1):
                there = (rr != r) if dc == 0 else col_exists(dc)

                @pl.when(there)
                def _():
                    level_copy(rr, dc, True).wait_recv()

        event_shift = jnp.where(lane >= blocks, capacity, 0)
        levels = []
        for kc in range(3):
            placed = jnp.where(
                row_id == 0, where_held[0, kc], jnp.where(row_id == 1, where_held[1, kc], where_held[2, kc])
            )
            source = lax.shift_right_logical(placed, capacity.bit_length() - 1)
            at = jnp.bitwise_and(placed, capacity - 1) + event_shift
            level = jnp.full(tile_shape, DRY_SECTION, jnp.float32)
            for rr in range(row_total):
                level = jnp.where(source == rr, pick_lanes(landed[rr, kc], at), level)
            levels.append(level)

        def block_at(e, t):
            dr, row = 0, t - halo_tiles
            if t < halo_tiles:
                dr, row = -1, block_rows - halo_tiles + t
            elif row >= own_tiles:
                dr, row = 1, row - own_tiles
            return dr, row, e * blocks + row * block_cols

        def set_surface(t):
            for e in range(events):
                dr, row, at = block_at(e, t)
                for j in range(cols):
                    value = SCALE * jnp.maximum(
                        level_of(levels[1], dr, at + j) - ext[0, span(t), piece(j)], 0.0
                    )
                    if dr == 0:
                        hand_depth[e, span(row), piece(j)] = value
                    rows[0, e, j, span(t), :] = value + bed_rows[j, span(t), :]

        def set_side_surface(t):
            side_height = beside(0, t)
            for e in range(events):
                dr, row, at = block_at(e, t)
                level = jnp.where(
                    near, level_of(levels[2], dr, at), level_of(levels[0], dr, at + block_cols - 1)
                )
                value = SCALE * jnp.maximum(level - side_height, 0.0) + bed_rows[cols, span(t), :]
                rows[0, e, cols, span(t), :] = jnp.where(lane_ok, value, 0.0)

        own_range = range(halo_tiles, halo_tiles + own_tiles)
        for t in own_range:
            set_surface(t)
        for index, (dr, dc) in enumerate(REGIONS):
            if dc == 0 or (dr == -1 and not has_north) or (dr == 1 and not has_south):
                continue

            @pl.when(col_exists(dc))
            def _():
                for array in range(3):
                    strip_copy(index, array, dr, dc).wait_recv()
        for t in row_tiles:
            set_terrain(t, True)
            set_side_surface(t)
        if shared:
            for array in range(3):
                for index, dr in halos:
                    pass_on(index, array, dr).wait_recv()
        for t in row_tiles:
            if t not in own_range:
                set_terrain(t, False)
                set_surface(t)

        base = 0
        for first, tiles, _ in plan:
            start = spread(bed_rows, first, tiles, 0)
            here = start
            for t in range(tiles):
                after = below(True, start) if t == tiles - 1 else spread(bed_rows, first, tiles, t + 1)
                fixed[base + t, 0] = here
                fixed[base + t, 1] = jnp.maximum(here, left(here))
                fixed[base + t, 2] = jnp.maximum(here, after)
                fixed[base + t, 3] = spread(drag_rows, first, tiles, t)
                here = after
            base += tiles
        def one_step(base, tiles, chosen):
            end = tiles - 1
            for e in chosen:
                def go_south(t, here, beyond):
                    return face(south[e, t], here, beyond, fixed[base + t, 2], fixed[base + t, 3])

                start = surface[e, 0]
                final_south = go_south(end, surface[e, end], below(True, start))
                above = down(final_south)
                if not has_north:
                    above = jnp.where(first_row, (fixed[base, 0] - start) * start, above)
                here = start
                for t in range(tiles):
                    if t == end:
                        new_south = final_south
                        after = None
                    else:
                        after = surface[e, t + 1]
                        new_south = go_south(t, here, after)
                    new_east = face(
                        east[e, t], here, left(here), fixed[base + t, 1], fixed[base + t, 3]
                    )
                    change = (right(new_east) - new_east) + (above - new_south)
                    surface[e, t] = guard(jnp.maximum(here + change, fixed[base + t, 0]))
                    east[e, t] = guard(new_east)
                    south[e, t] = new_south
                    above = new_south
                    here = after

        base = 0
        for number, (first, tiles, steps) in enumerate(plan):
            if number > 0:
                old_first, old_tiles, _ = plan[number - 1]
                for e in range(events):
                    for which, ref in enumerate((surface, east, south)):
                        for t in range(old_tiles):
                            gather_back(rows.at[which, e], old_first, old_tiles, t, ref[e, t])
            for e in range(events):
                for which, ref in enumerate((surface, east, south)):
                    if number > 0 or which == 0:
                        for t in range(tiles):
                            ref[e, t] = spread(rows.at[which, e], first, tiles, t)

            def one(turn, carry, base=base, tiles=tiles):
                one_step(base, tiles, range(events))
                return carry

            def one_apart(turn, carry, base=base, tiles=tiles):
                one_step(base, tiles, (lax.rem(turn, events),))
                return carry

            if tiles <= TOGETHER_TILES:
                lax.fori_loop(0, steps, one, 0)
            else:
                lax.fori_loop(0, steps * events, one_apart, 0)
            base += tiles
        first, tiles, _ = plan[-1]
        for e in range(events):
            for t in range(tiles):
                gather_back(rows.at[0, e], first, tiles, t, surface[e, t])
            for t in range(own_tiles):
                for j in range(cols):
                    at = span(halo_tiles + t)
                    final_depth[e, span(t), piece(j)] = rows[0, e, j, at, :] - bed_rows[j, at, :]

    for copy in own_copies:
        copy.wait()

    @pl.when(r == 0)
    def _():
        flood(False, True)

    @pl.when(jnp.logical_and(r > 0, r < row_total - 1))
    def _():
        flood(True, True)

    @pl.when(r == row_total - 1)
    def _():
        flood(True, False)

    if shared:
        for index, dr in tall:
            @pl.when(row_exists(dr))
            def _():
                for array in range(3):
                    pass_on(index, array, dr).wait_send()
    for index, (dr, dc) in enumerate(REGIONS):
        @pl.when(tile_exists(-dr, -dc))
        def _():
            place_copy(index, dr, dc).wait_send()
            for array in range(3):
                strip_copy(index, array, dr, dc).wait_send()
    for rr in range(row_total):
        for dc in (-1, 0, 1):
            there = (rr != r) if dc == 0 else col_exists(dc)

            @pl.when(there)
            def _():
                level_copy(rr, dc, False).wait_send()


def body(
    row_total, col_total, cores,
    sections, send_list, send_count, slot_sender_position, block_slot_index, hand, drain, manning,
):
    events = sections.shape[0]
    tile_rows, tile_cols = hand.shape
    vmem = pl.BlockSpec(memory_space=pltpu.VMEM)
    hbm = pl.BlockSpec(memory_space=pltpu.HBM)
    padded_rows = tile_rows + 2 * HALO
    padded_tiles = padded_rows // SUBLANES
    width = tile_cols + LANES
    pieces = width // LANES
    small = (sections, send_list, send_count, slot_sender_position, block_slot_index)
    list_rows = -(-row_total // SUBLANES) * SUBLANES
    fixed_tiles = max(
        sum(tiles for tiles, _ in EDGE_STEPS), sum(tiles for tiles, _ in INNER_STEPS)
    )
    by_rows = pltpu.VMEM((pieces, padded_rows, LANES), jnp.float32)
    state = pltpu.VMEM((events, padded_tiles, SUBLANES, width), jnp.float32)
    out = jax.ShapeDtypeStruct((events, tile_rows, tile_cols), jnp.float32)
    start, end = pl.pallas_call(
        functools.partial(flood_kernel, row_total, col_total, cores),
        out_shape=(out, out),
        in_specs=[hbm] * 8,
        out_specs=(vmem, vmem),
        scratch_shapes=[pltpu.VMEM(x.shape, x.dtype) for x in small]
        + [
            pltpu.VMEM((3, padded_rows, tile_cols + 2 * LANES), jnp.float32),
            pltpu.VMEM((list_rows, LANES), jnp.int32),
            pltpu.VMEM((SUBLANES, LANES), jnp.int32),
            pltpu.VMEM((SUBLANES, LANES), jnp.int32),
            pltpu.VMEM((row_total, SUBLANES, LANES), jnp.float32),
            pltpu.VMEM((row_total, 3, SUBLANES, LANES), jnp.float32),
            pltpu.VMEM((SUBLANES, LANES), jnp.int32),
            pltpu.VMEM((3, 3, SUBLANES, LANES), jnp.int32),
            by_rows,
            by_rows,
            pltpu.VMEM((3, events, pieces, padded_rows, LANES), jnp.float32),
            state,
            state,
            state,
            pltpu.VMEM((fixed_tiles, 4, SUBLANES, width), jnp.float32),
            pltpu.SemaphoreType.DMA((len(small),)),
            pltpu.SemaphoreType.DMA((3,)),
            pltpu.SemaphoreType.DMA((len(REGIONS), 3)),
            pltpu.SemaphoreType.DMA((len(REGIONS), 3)),
            pltpu.SemaphoreType.DMA((row_total, 3)),
            pltpu.SemaphoreType.DMA((row_total, 3)),
            pltpu.SemaphoreType.DMA((len(REGIONS),)),
            pltpu.SemaphoreType.DMA((len(REGIONS),)),
            pltpu.SemaphoreType.DMA((len(REGIONS), 3)),
            pltpu.SemaphoreType.DMA((len(REGIONS), 3)),
            pltpu.SemaphoreType.REGULAR,
            pltpu.SemaphoreType.REGULAR((row_total,)),
            pltpu.SemaphoreType.REGULAR,
        ],
        compiler_params=pltpu.CompilerParams(
            collective_id=0, has_side_effects=True, vmem_limit_bytes=VMEM_BYTES
        ),
        name="flood",
    )(*[pltpu.with_memory_space_constraint(x, pltpu.HBM) for x in (*small, hand, drain, manning)])
    return start * (1.0 / SCALE), end * (1.0 / SCALE)


def solution(mesh):
    return jax.shard_map(
        functools.partial(body, mesh.shape["row"], mesh.shape["col"], mesh.shape["evt"]),
        mesh=mesh,
        in_specs=(
            P("evt", ("grp", "row", "col")),
            P(("grp", "row"), "col", None, None),
            P(("grp", "row"), "col", None),
            P(("grp", "row"), "col", None),
            P(("grp", "row"), "col"),
            P(("grp", "row"), "col"),
            P(("grp", "row"), "col"),
            P(("grp", "row"), "col"),
        ),
        out_specs=(P("evt", ("grp", "row"), "col"), P("evt", ("grp", "row"), "col")),
        check_vma=False,
    )
```
